256 devices in a mesh: blk: 8 (over y, x_hi), dp: 32 (over x_lo, z, core).
Axes of the slice: x: 4 (x_hi: 2, x_lo: 2; x = x_hi * 2 + x_lo), y: 4, z: 8, core: 2. Of those that a mesh axis runs over, the one named last changes fastest.
Arguments:
- patches: bfloat16 [32768, 64, 256], P(('blk', 'dp')), may hold values from -6 to 6
- w_mix: bfloat16 [256, 128], replicated, may hold values from -0.375 to 0.375
- w_in: bfloat16 [2048, 512], replicated, may hold values from -0.125 to 0.125
- w_out: bfloat16 [512, 128], replicated, may hold values from -0.25 to 0.25
- partner_dev: int32 [32768], P(('blk', 'dp')), may hold values from 0 to 31, as said below
- partner_row: int32 [32768], P(('blk', 'dp')), may hold values from 0 to 127, as said below
Outputs:
- loss_rows: float32 [32768], P(('blk', 'dp'))
- grad_mix: float32 [256, 128], replicated
- grad_in: float32 [2048, 512], replicated
- grad_out: float32 [512, 128], replicated
The draws below stay inside these ranges and needn't reach their ends.
Inputs may be any that keep to these rules, and one draw needn't show every extreme that they name: Among one device's rows every dp index appears as partner_dev exactly 128/32 times. Over the rows that share a blk index, the pairs (partner_dev, partner_row) name every pair of dp index and row of a device exactly once.
All inputs are finite; a program needn't handle non-finite values.
Results may differ from the reference program's by a relative error of at most 0.012.
The reference program's roundings to bfloat16 on the way count: a program that leaves them out, or rounds other values in their place, can miss the bound.
Values may be sent and summed in bfloat16 or wider, within the bound.
A program may use at most 64 MiB of HBM per device.

```python
import math
import jax
import jax.numpy as jnp
from jax import lax

ANGLES = 64
FILTERS = 128
HIDDEN_SIZE = 512
EMBED = 128
PATCHES = 128
LANES = 256
FEATS = 2048
PEERS = 32
CYCLE = 8
ROWS = 32768
N_BLK = 8
N_DP = 32


def partner_table(key):
    base = jax.random.fold_in(key, 17)
    per_peer = PATCHES // PEERS

    def one_cycle(subkey):
        send_key, recv_key = jax.random.split(subkey)
        send_perm = jax.vmap(lambda each: jax.random.permutation(each, PATCHES))(jax.random.split(send_key, PEERS))
        recv_perm = jax.vmap(lambda each: jax.random.permutation(each, PATCHES))(jax.random.split(recv_key, PEERS))
        sender_index = jnp.broadcast_to(jnp.arange(PEERS, dtype=jnp.int32)[:, None], (PEERS, PATCHES))
        slot = jnp.broadcast_to(jnp.arange(PATCHES, dtype=jnp.int32)[None, :], (PEERS, PATCHES))
        target = jnp.mod(sender_index + slot // per_peer, PEERS)
        target_row = recv_perm[target, slot]
        devices = jnp.zeros((PEERS, PATCHES), jnp.int32).at[sender_index, send_perm].set(target)
        rows_out = jnp.zeros((PEERS, PATCHES), jnp.int32).at[sender_index, send_perm].set(target_row)
        return (devices, rows_out)
    devices, rows_out = jax.vmap(one_cycle)(jax.random.split(base, CYCLE))
    return (devices.reshape(-1), rows_out.reshape(-1))


def draw_partner_dev(key, part):
    return partner_table(key)[0]


def draw_partner_row(key, part):
    return partner_table(key)[1]


def levels(stream_key, shape, cuts, least, top_value):
    def one(dim, shards_of):
        steps = jax.random.uniform(jax.random.fold_in(jax.random.fold_in(stream_key, 6), dim), (shards_of,), jnp.float32, least / len(cuts), top_value / len(cuts))
        return jnp.repeat(jnp.exp(steps), shape[dim] // shards_of).reshape((-1,) + (1,) * (len(shape) - dim - 1))

    factor_of = one(*cuts[0])
    for cut in cuts[1:]:
        factor_of = factor_of * one(*cut)
    return factor_of


def scatter_about(key, dims, scale, limit, pieces=(), kind=jnp.bfloat16):
    gain = levels(key, dims, pieces, -0.22, 0.18) if pieces else 1.0
    values = jax.random.normal(key, dims, jnp.float32) * scale * gain
    return jnp.minimum(jnp.maximum(values, -limit), limit).astype(kind)


def setup_inputs(seed: int = 0) -> dict:
    key_list = jax.random.split(jax.random.key(seed), 7)
    patches = scatter_about(key_list[0], (ROWS, ANGLES, LANES), 1.0, 6.0, ((0, 256),))
    w_mix = scatter_about(key_list[1], (LANES, FILTERS), LANES ** -0.5, 0.375)
    w_in = scatter_about(key_list[2], (FEATS, HIDDEN_SIZE), FEATS ** -0.5, 0.125)
    w_out = scatter_about(key_list[3], (HIDDEN_SIZE, EMBED), HIDDEN_SIZE ** -0.5, 0.25)
    partner_dev = draw_partner_dev(jax.random.fold_in(key_list[6], 71), 0)
    partner_row = draw_partner_row(jax.random.fold_in(key_list[6], 71), 0)
    return dict(patches=patches, w_mix=w_mix, w_in=w_in, w_out=w_out, partner_dev=partner_dev, partner_row=partner_row)


SCALE = 10.0

def dft_table(length, freqs):
    angle_idx = jnp.arange(length, dtype=jnp.int32)
    freq_idx = jnp.arange(freqs, dtype=jnp.int32)
    phase = jnp.mod(freq_idx[None, :] * angle_idx[:, None], length).astype(jnp.float32) * (2.0 * math.pi / length)
    return jnp.concatenate([jnp.cos(phase), -jnp.sin(phase)], axis=1).astype(jnp.bfloat16)

def encode(block, w_mix, w_in, w_out):
    count, length, lanes = block.shape
    filters = w_mix.shape[1]
    freqs = w_in.shape[0] // filters
    angle_table = dft_table(length, freqs)
    spec = jnp.einsum('pac,ak->pkc', block.astype(jnp.float32), angle_table.astype(jnp.float32), precision=lax.Precision.HIGHEST).astype(jnp.bfloat16)
    mixed = jnp.dot(spec.reshape(-1, lanes), w_mix, preferred_element_type=jnp.float32).reshape(count, 2 * freqs, filters)
    real_part = mixed[:, :freqs]
    imag_part = mixed[:, freqs:]
    powers = real_part * real_part + imag_part * imag_part
    features = jnp.log1p(powers).reshape(count, -1)
    mean_removed = features - lax.optimization_barrier(jnp.mean(features, axis=1, keepdims=True))
    reciprocal_scale = lax.rsqrt(lax.optimization_barrier(jnp.mean(mean_removed * mean_removed, axis=1, keepdims=True)) + 1e-05)
    normed = (mean_removed * reciprocal_scale).astype(jnp.bfloat16)
    preact = jnp.dot(normed, w_in, preferred_element_type=jnp.float32)
    hidden = jax.nn.silu(preact).astype(jnp.bfloat16)
    raw_embed = jnp.dot(hidden, w_out, preferred_element_type=jnp.float32)
    norms = jnp.sqrt(lax.optimization_barrier(jnp.sum(raw_embed * raw_embed, axis=1, keepdims=True)) + 1e-06)
    unit32 = raw_embed / norms
    saved = (spec, real_part, imag_part, powers, mean_removed, reciprocal_scale, normed, preact, hidden, unit32, norms)
    return (unit32.astype(jnp.bfloat16), saved)

def encode_back(grad_units, saved, w_in, w_out):
    spec, real_part, imag_part, powers, mean_removed, reciprocal_scale, normed, preact, hidden, unit32, norms = saved
    count = spec.shape[0]
    lanes = spec.shape[2]
    grad_raw = ((grad_units - unit32 * lax.optimization_barrier(jnp.sum(unit32 * grad_units, axis=1, keepdims=True))) / norms).astype(jnp.bfloat16)
    g_out = jnp.dot(hidden.T, grad_raw, preferred_element_type=jnp.float32)
    grad_hid = jnp.dot(grad_raw, w_out.T, preferred_element_type=jnp.float32)
    sigm = jax.nn.sigmoid(preact)
    grad_pre = (grad_hid * sigm * (1.0 + preact * (1.0 - sigm))).astype(jnp.bfloat16)
    g_in = jnp.dot(normed.T, grad_pre, preferred_element_type=jnp.float32)
    norm_gradient = jnp.dot(grad_pre, w_in.T, preferred_element_type=jnp.float32)
    normalized_input = mean_removed * reciprocal_scale
    feature_gradient = reciprocal_scale * (norm_gradient - lax.optimization_barrier(jnp.mean(norm_gradient, axis=1, keepdims=True)) - normalized_input * lax.optimization_barrier(jnp.mean(norm_gradient * normalized_input, axis=1, keepdims=True)))
    grad_pow = feature_gradient.reshape(powers.shape) / (1.0 + powers)
    grad_mixed = jnp.concatenate([2.0 * real_part * grad_pow, 2.0 * imag_part * grad_pow], axis=1).astype(jnp.bfloat16)
    g_mix = jnp.dot(spec.reshape(-1, lanes).T, grad_mixed.reshape(-1, grad_mixed.shape[2]), preferred_element_type=jnp.float32)
    return (g_mix, g_in, g_out)

def group_terms(pair):
    key_rows, spos = pair
    scores = SCALE * jnp.dot(key_rows, key_rows.T, preferred_element_type=jnp.float32)
    width = key_rows.shape[0]
    diagonal = jnp.arange(width)[:, None] == jnp.arange(width)[None, :]
    expo = jnp.where(diagonal, jnp.float32(0.0), jnp.exp(scores))
    zneg = lax.optimization_barrier(jnp.sum(expo, axis=1))
    totals = jnp.exp(spos) + zneg
    numer = jnp.dot(expo.astype(jnp.bfloat16), key_rows, preferred_element_type=jnp.float32)
    weights = (expo / totals[:, None]).astype(jnp.bfloat16)
    keyterm = jnp.dot(weights.T, key_rows, preferred_element_type=jnp.float32)
    return (totals, numer, keyterm)

def reference(patches, w_mix, w_in, w_out, partner_dev, partner_row):
    blocks = patches.reshape(N_BLK * N_DP, PATCHES, ANGLES, LANES)
    units = lax.map(lambda block: encode(block, w_mix, w_in, w_out)[0], blocks)
    units4 = units.reshape(N_BLK, N_DP, PATCHES, EMBED)
    peer_dev = partner_dev.reshape(N_BLK, N_DP, PATCHES)
    peer_row = partner_row.reshape(N_BLK, N_DP, PATCHES)
    blk_ids = jnp.broadcast_to(jnp.arange(N_BLK, dtype=jnp.int32)[:, None, None], peer_dev.shape)
    positive = units4[blk_ids, peer_dev, peer_row]
    spos = SCALE * lax.optimization_barrier(jnp.sum(units4.astype(jnp.float32) * positive.astype(jnp.float32), axis=-1))
    grouped = jnp.transpose(units4, (1, 0, 2, 3)).reshape(N_DP, N_BLK * PATCHES, EMBED)
    spos_grouped = jnp.transpose(spos, (1, 0, 2)).reshape(N_DP, N_BLK * PATCHES)
    totals, numer, keyterm = lax.map(group_terms, (grouped, spos_grouped))
    totals = jnp.transpose(totals.reshape(N_DP, N_BLK, PATCHES), (1, 0, 2))
    numer = jnp.transpose(numer.reshape(N_DP, N_BLK, PATCHES, EMBED), (1, 0, 2, 3))
    keyterm = jnp.transpose(keyterm.reshape(N_DP, N_BLK, PATCHES, EMBED), (1, 0, 2, 3))
    loss_rows = (jnp.log(totals) - spos).reshape(-1)
    coef = SCALE / PATCHES
    ppos = jnp.exp(spos) / totals
    partner_grad = coef * (ppos - 1.0)[..., None] * units4.astype(jnp.float32)
    from_partner = jnp.zeros(units4.shape, jnp.float32).at[blk_ids, peer_dev, peer_row].add(partner_grad)
    grad_units = coef * ((ppos - 1.0)[..., None] * positive.astype(jnp.float32) + numer / totals[..., None]) + coef * keyterm + from_partner
    grad_units = grad_units.reshape(N_BLK * N_DP, PATCHES, EMBED)

    def accumulate(carry, pair):
        block, grad_block = pair
        unused, saved = encode(block, w_mix, w_in, w_out)
        g_mix, g_in, g_out = encode_back(grad_block, saved, w_in, w_out)
        return ((carry[0] + g_mix, carry[1] + g_in, carry[2] + g_out), None)
    start = (jnp.zeros((LANES, FILTERS), jnp.float32), jnp.zeros((FEATS, HIDDEN_SIZE), jnp.float32), jnp.zeros((HIDDEN_SIZE, EMBED), jnp.float32))
    sums, unused = lax.scan(accumulate, start, (blocks, grad_units))
    return (loss_rows, sums[0], sums[1], sums[2])
```

```python
import functools
import math

import jax
import jax.numpy as jnp
import ml_dtypes
import numpy as np
from jax import lax
from jax.experimental import pallas as pl
from jax.experimental.pallas import tpu as pltpu
from jax.sharding import PartitionSpec as P

SCALE = 10.0
MESH = pl.DeviceIdType.MESH
F32 = jnp.float32
BF16 = jnp.bfloat16

COUNT = 128
ANGLES = 64
LANES = 256
FREQS = 16
FILTERS = 128
FEATS = FREQS * FILTERS
HIDDEN = 512
EMBED = 128
PEERS = 32
CYCLE = 8
GROUP = CYCLE * COUNT
SLOT = 8
SMALL = 384
COEF = SCALE / COUNT


def block_table():
    angle = np.arange(ANGLES)
    freq = np.arange(FREQS)
    phase = np.mod(freq[None, :] * angle[:, None], ANGLES).astype(np.float32) * np.float32(
        2.0 * math.pi / ANGLES
    )
    table = np.concatenate([np.cos(phase), -np.sin(phase)], axis=1)
    wide = np.zeros((2 * FREQS, 8, 8, ANGLES), np.float32)
    for n in range(8):
        wide[:, n, n, :] = table.T
    return wide.reshape(2 * FREQS * 8, 8 * ANGLES).astype(ml_dtypes.bfloat16)


def dot(a, b):
    return jnp.dot(a, b, preferred_element_type=F32)


def dot_t(a, b):
    return lax.dot_general(a, b, (((1,), (1,)), ((), ())), preferred_element_type=F32)


def split(v):
    high = v.astype(BF16)
    return high, (v - high.astype(F32)).astype(BF16)


def iota(shape, dim):
    return lax.broadcasted_iota(jnp.int32, shape, dim)


def kernel(
    pdev_ref, prow_ref, table_hbm, wmix_hbm, win_hbm, wout_hbm, patches_hbm,
    loss_ref, big_ref, small_ref,
    patches, table, wmix, win, wout,
    spec, spec_t, real, imag, feat, normed, preact, hid_t, ngrad, mixg,
    group, ask_out, ask_in, row_out, row_in, back_out, back_in, tot_all,
    nt_own, nt_send, nt_sib, gp_own, gp_sib,
    pa, pb, ra1, rb1, pa2, pb2, ra2, rb2, pa3, pb3, ra3, rb3,
    sm, sm_sib, sm0, sz, sx, sy,
    load_sem, send_sem, recv_sem,
):
    blk = lax.axis_index("blk")
    dp = lax.axis_index("dp")
    y = blk // 2
    x = (blk % 2) * 2 + dp // 16
    z = (dp // 2) % 8
    core = dp % 2
    other = 1 - core

    def device(x_, y_, z_, c_):
        return (y_ * 2 + x_ // 2, ((x_ % 2) * 8 + z_) * 2 + c_)

    sibling = device(x, y, z, other)

    def dp_peer(i):
        quad = i // 4
        half = (quad + 1) // 2
        dz = 4 + half * (2 * (quad % 2) - 1)
        xl = (dp // 16 + 1 - (i % 4) // 2) % 2
        c = (core + 1 - i % 2) % 2
        return (xl * 8 + (z + dz) % 8) * 2 + c

    used = [0]
    started = []

    def remote(src, dst, to):
        k = used[0]
        used[0] += 1
        copy = pltpu.make_async_remote_copy(
            src_ref=src, dst_ref=dst, send_sem=send_sem.at[k], recv_sem=recv_sem.at[k],
            device_id=to, device_id_type=MESH,
        )
        copy.start()
        started.append(copy)
        return copy

    def spread(src, dst):
        k = used[0]
        used[0] += 1
        mine = pl.multiple_of(dp * SLOT, SLOT)

        def send(i, carry):
            p = dp_peer(i)
            pltpu.make_async_remote_copy(
                src_ref=src.at[pl.ds(pl.multiple_of(p * SLOT, SLOT), SLOT)],
                dst_ref=dst.at[pl.ds(mine, SLOT)],
                send_sem=send_sem.at[k], recv_sem=recv_sem.at[k],
                device_id=(blk, p), device_id_type=MESH,
            ).start()
            return carry

        lax.fori_loop(0, PEERS - 1, send, 0)
        dst[pl.ds(mine, SLOT), :] = src[pl.ds(mine, SLOT), :]
        rows = pl.ds(0, (PEERS - 1) * SLOT)
        whole = pltpu.make_async_remote_copy(
            src_ref=src.at[rows], dst_ref=dst.at[rows], send_sem=send_sem.at[k],
            recv_sem=recv_sem.at[k], device_id=(blk, dp_peer(0)), device_id_type=MESH,
        )
        started.append(whole)
        return whole

    def to_group(ref, rows):
        k = used[0]
        used[0] += 1
        mine = pl.ds(pl.multiple_of(blk * rows, rows), rows)
        for step in (5, 4, 3, 2, 1, 6, 7):
            pltpu.make_async_remote_copy(
                src_ref=ref.at[mine], dst_ref=ref.at[mine],
                send_sem=send_sem.at[k], recv_sem=recv_sem.at[k],
                device_id=((blk + step) % CYCLE, dp), device_id_type=MESH,
            ).start()
        span = pl.ds(0, (CYCLE - 1) * rows)
        whole = pltpu.make_async_remote_copy(
            src_ref=ref.at[span], dst_ref=ref.at[span], send_sem=send_sem.at[k],
            recv_sem=recv_sem.at[k], device_id=((blk + 1) % CYCLE, dp), device_id_type=MESH,
        )
        started.append(whole)
        return whole

    chunk = 1024
    loads = [pltpu.make_async_copy(table_hbm, table, load_sem.at[0])]
    for g in range(8):
        rows = pl.ds(g * chunk, chunk)
        loads.append(pltpu.make_async_copy(patches_hbm.at[rows], patches.at[rows], load_sem.at[1 + g]))
    loads.append(pltpu.make_async_copy(wmix_hbm, wmix, load_sem.at[9]))
    loads.append(pltpu.make_async_copy(win_hbm, win, load_sem.at[10]))
    loads.append(pltpu.make_async_copy(wout_hbm, wout, load_sem.at[11]))
    for load in loads:
        load.start()

    barrier = pltpu.get_barrier_semaphore()

    def greet(i, carry):
        pl.semaphore_signal(barrier, inc=1, device_id=(blk, dp_peer(i)), device_id_type=MESH)
        return carry

    lax.fori_loop(0, PEERS - 1, greet, 0)
    for step in range(1, CYCLE):
        pl.semaphore_signal(barrier, inc=1, device_id=((blk + step) % CYCLE, dp), device_id_type=MESH)
    pl.semaphore_signal(barrier, inc=1, device_id=device(3 - x, y, z, core), device_id_type=MESH)

    lane = iota((COUNT, COUNT), 1)
    row = iota((COUNT, COUNT), 0)
    dev_lane = jnp.broadcast_to(pdev_ref[...], (COUNT, COUNT))
    dev_row = dev_lane.astype(F32).T.astype(jnp.int32)
    same = dev_lane == dev_row
    rank_lane = jnp.sum(jnp.where(same & (row < lane), 1.0, 0.0), axis=0, keepdims=True)
    rank_row = jnp.sum(jnp.where(same & (lane < row), 1.0, 0.0), axis=1, keepdims=True)
    place_lane = pdev_ref[...] * SLOT + rank_lane.astype(jnp.int32)
    place_row = dev_row[:, :1] * SLOT + rank_row.astype(jnp.int32)
    to_slot = jnp.where(
        iota((PEERS * SLOT, COUNT), 0) == place_lane, 1.0, 0.0
    ).astype(BF16)
    from_slot = jnp.where(
        iota((COUNT, PEERS * SLOT), 1) == place_row, 1.0, 0.0
    ).astype(BF16)
    prow = jnp.broadcast_to(prow_ref[...], (COUNT, COUNT)).astype(F32).T.astype(BF16)
    ask_out[...] = dot(to_slot, prow)

    pl.semaphore_wait(barrier, PEERS - 1 + CYCLE - 1 + 1)
    asked = spread(ask_out, ask_in)

    loads[0].wait()
    bank = table[...]
    for g in range(8):
        loads[1 + g].wait()
        low = dot(bank, patches[g * chunk : g * chunk + 512, :])
        high = dot(bank, patches[g * chunk + 512 : (g + 1) * chunk, :])
        for k in range(2 * FREQS):
            part = jnp.concatenate([low[k * 8 : k * 8 + 8], high[k * 8 : k * 8 + 8]], axis=0)
            spec[k * COUNT + g * 16 : k * COUNT + g * 16 + 16, :] = part.astype(BF16)

    loads[9].wait()
    total = jnp.zeros((COUNT, 1), F32)
    for k in range(0, FREQS, 4):
        rows = slice(k * COUNT, (k + 4) * COUNT)
        re = dot(spec[rows, :], wmix[...])
        im = dot(spec[(FREQS + k) * COUNT : (FREQS + k + 4) * COUNT, :], wmix[...])
        real[rows, :] = re
        imag[rows, :] = im
        value = jnp.log1p(re * re + im * im)
        acc = jnp.zeros((COUNT, FILTERS), F32)
        for i in range(4):
            piece = value[i * COUNT : (i + 1) * COUNT]
            feat[:, (k + i) * FILTERS : (k + i + 1) * FILTERS] = piece
            acc = acc + piece
        total = total + jnp.sum(acc, axis=1, keepdims=True)
    mean = total * (1.0 / FEATS)
    acc = jnp.zeros((COUNT, FILTERS), F32)
    for k in range(FREQS):
        off = feat[:, k * FILTERS : (k + 1) * FILTERS] - mean
        acc = acc + off * off
    rscale = lax.rsqrt(jnp.sum(acc, axis=1, keepdims=True) * (1.0 / FEATS) + 1e-05)
    for k in range(FREQS):
        cols = slice(k * FILTERS, (k + 1) * FILTERS)
        hat = (feat[:, cols] - mean) * rscale
        feat[:, cols] = hat
        normed[:, cols] = hat.astype(BF16)

    loads[10].wait()
    pre = dot(normed[...], win[...])
    preact[...] = pre
    hidden = (pre * jax.nn.sigmoid(pre)).astype(BF16)
    loads[11].wait()
    raw = dot(hidden, wout[...])
    norms = jnp.sqrt(jnp.sum(raw * raw, axis=1, keepdims=True) + 1e-06)
    unit32 = raw / norms
    units = unit32.astype(BF16)
    group[pl.ds(pl.multiple_of(blk * COUNT, COUNT), COUNT), :] = units
    gathered = to_group(group, COUNT)

    asked.wait_recv()
    wanted = ask_in[...]
    valid = iota((PEERS * SLOT, COUNT), 0) % SLOT < SLOT // 2
    pick32 = jnp.where(
        valid & (wanted == iota((PEERS * SLOT, COUNT), 1).astype(F32)), 1.0, 0.0
    )
    pick = pick32.astype(BF16)
    row_out[...] = dot(pick, units)
    returned = spread(row_out, row_in)

    unpick = pick32.T.astype(BF16)
    base = core * (FEATS // 2)
    for k in range(8):
        cols = pl.ds(pl.multiple_of((1 - core) * (FEATS // 2) + k * FILTERS, FILTERS), FILTERS)
        nt_send[k * FILTERS : (k + 1) * FILTERS, :] = normed[:, cols].T
    factor = remote(nt_send, nt_sib, sibling)
    for k in range(8):
        cols = pl.ds(pl.multiple_of(base + k * FILTERS, FILTERS), FILTERS)
        nt_own[k * FILTERS : (k + 1) * FILTERS, :] = normed[:, cols].T
    hid_t[...] = hidden.T
    for k in range(2 * FREQS):
        spec_t[:, k * COUNT : (k + 1) * COUNT] = spec[k * COUNT : (k + 1) * COUNT, :].T

    gathered.wait_recv()
    keys = group[...]
    scores = SCALE * dot_t(units, keys)
    self_lane = blk * COUNT + iota((COUNT, GROUP), 0)
    expo = jnp.where(iota((COUNT, GROUP), 1) == self_lane, 0.0, jnp.exp(scores))
    zneg = jnp.sum(expo, axis=1, keepdims=True)
    numer = dot(expo.astype(BF16), keys)

    returned.wait_recv()
    positive = dot(from_slot, row_in[...].astype(BF16))
    own = units.astype(F32)
    spos = SCALE * jnp.sum(own * positive, axis=1, keepdims=True)
    epos = jnp.exp(spos)
    totals = epos + zneg
    tot_lane = jnp.broadcast_to(totals, (COUNT, COUNT)).T
    tot_all[pl.ds(pl.multiple_of(blk * SLOT, SLOT), SLOT), :] = tot_lane[:SLOT]
    tots = to_group(tot_all, SLOT)
    away = COEF * (epos / totals - 1.0)
    high, low = split(away * own)
    back_out[...] = dot(to_slot, high) + dot(to_slot, low)
    backs = spread(back_out, back_in)
    spos_lane = jnp.broadcast_to(spos, (COUNT, COUNT)).T
    loss_ref[...] = (jnp.log(tot_lane) - spos_lane)[:1]
    grad_units = away * positive + COEF * (numer / totals)

    tots.wait_recv()
    inverse = jnp.concatenate(
        [1.0 / tot_all[b * SLOT : b * SLOT + 1, :] for b in range(CYCLE)], axis=1
    )
    keyterm = dot((expo * inverse).astype(BF16), keys)
    grad_units = grad_units + COEF * keyterm
    backs.wait_recv()
    high, low = split(back_in[...])
    grad_units = grad_units + (dot(unpick, high) + dot(unpick, low))

    grad_raw = (
        (grad_units - unit32 * jnp.sum(unit32 * grad_units, axis=1, keepdims=True)) / norms
    ).astype(BF16)
    grad_hid = dot_t(grad_raw, wout[...])
    pre = preact[...]
    sigm = jax.nn.sigmoid(pre)
    grad_pre = (grad_hid * sigm * (1.0 + pre * (1.0 - sigm))).astype(BF16)
    gp_own[...] = grad_pre
    sent = remote(gp_own, gp_sib, sibling)
    g_out = dot(hid_t[...], grad_raw)
    sm[0, 0:256, :] = g_out[:256]
    sm[1, 0:256, :] = g_out[256:]
    ngrad[...] = dot_t(grad_pre, win[...])

    factor.wait_recv()
    sent.wait_recv()
    right = jnp.concatenate([gp_own[...], gp_sib[...]], axis=0)
    for i in range(4):
        rows = slice(i * 256, (i + 1) * 256)
        prod = dot(jnp.concatenate([nt_own[rows, :], nt_sib[rows, :]], axis=1), right).astype(BF16)
        pa[i * 256 : (i + 1) * 256, :] = prod[:, 0:128]
        pa[1024 + i * 256 : 1024 + (i + 1) * 256, :] = prod[:, 128:256]
        pb[i * 256 : (i + 1) * 256, :] = prod[:, 256:384]
        pb[1024 + i * 256 : 1024 + (i + 1) * 256, :] = prod[:, 384:512]

    def x_peer(k):
        return device((x + k) % 4, y, z, core)

    def y_peer(k):
        return device(x, (y + k) % 4, z, core)

    def z_peer(k):
        return device(x, y, (z + k) % 8, core)

    def piece(at, rows):
        return pl.ds(pl.multiple_of(at * rows, rows), rows)

    a1 = {}
    b1 = {}
    for k in (2, 1, 3):
        a1[k] = remote(pa.at[piece((x + k) % 4, 512)], ra1.at[k - 1], x_peer(k))
        b1[k] = remote(pb.at[piece((y + k) % 4, 512)], rb1.at[k - 1], y_peer(k))

    acc = jnp.zeros((COUNT, FILTERS), F32)
    acc_hat = jnp.zeros((COUNT, FILTERS), F32)
    for k in range(FREQS):
        cols = slice(k * FILTERS, (k + 1) * FILTERS)
        ng = ngrad[:, cols]
        acc = acc + ng
        acc_hat = acc_hat + ng * feat[:, cols]
    mean_ng = jnp.sum(acc, axis=1, keepdims=True) * (1.0 / FEATS)
    mean_hat = jnp.sum(acc_hat, axis=1, keepdims=True) * (1.0 / FEATS)
    for k in range(FREQS):
        cols = slice(k * FILTERS, (k + 1) * FILTERS)
        rows = slice(k * COUNT, (k + 1) * COUNT)
        re = real[rows, :]
        im = imag[rows, :]
        grad_feat = rscale * (ngrad[:, cols] - mean_ng - feat[:, cols] * mean_hat)
        grad_pow = 2.0 * grad_feat / (1.0 + (re * re + im * im))
        mixg[rows, :] = (re * grad_pow).astype(BF16)
        mixg[(FREQS + k) * COUNT : (FREQS + k + 1) * COUNT, :] = (im * grad_pow).astype(BF16)
    g_mix = dot(spec_t[...], mixg[...])
    sm[0, 256:384, :] = g_mix[:128]
    sm[1, 256:384, :] = g_mix[128:]
    halves = remote(sm.at[other], sm_sib, sibling)

    def add(own_part, got, copies):
        value = own_part.astype(F32)
        for k in sorted(copies):
            copies[k].wait_recv()
            value = value + got[k - 1].astype(F32)
        return value.astype(BF16)

    pa2[...] = add(pa[piece(x, 512), :], ra1, a1)
    a2 = {k: remote(pa2.at[piece((y + k) % 4, 128)], ra2.at[k - 1], y_peer(k)) for k in (2, 1, 3)}
    pb2[...] = add(pb[piece(y, 512), :], rb1, b1)
    b2 = {k: remote(pb2.at[piece((x + k) % 4, 128)], rb2.at[k - 1], x_peer(k)) for k in (2, 1, 3)}

    halves.wait_recv()
    sm0[...] = (sm[core] + sm_sib[...]).astype(BF16)
    far = (4, 3, 5, 2, 6, 1, 7)
    s1 = {k: remote(sm0.at[piece((z + k) % 8, 48)], sz.at[k - 1], z_peer(k)) for k in far}

    pa3[...] = add(pa2[piece(y, 128), :], ra2, a2)
    a3 = {k: remote(pa3.at[piece((z + k) % 8, 16)], ra3.at[k - 1], z_peer(k)) for k in far}
    pb3[...] = add(pb2[piece(x, 128), :], rb2, b2)
    b3 = {k: remote(pb3.at[piece((z + k) % 8, 16)], rb3.at[k - 1], z_peer(k)) for k in far}

    sx[x] = add(sm0[piece(z, 48), :], sz, s1)
    s2 = [remote(sx.at[x], sx.at[x], x_peer(k)) for k in (2, 1, 3)]

    a_own = x * 512 + y * 128
    b_own = y * 512 + x * 128

    def span(at, rows):
        return pl.ds(pl.multiple_of(at, rows), rows)

    big_ref[core, 0, span(a_own + z * 16, 16), :] = add(pa3[piece(z, 16), :], ra3, a3)
    here = big_ref.at[core, 0, span(a_own + z * 16, 16)]
    a4 = [remote(here, here, z_peer(k)) for k in far]
    big_ref[core, 1, span(b_own + z * 16, 16), :] = add(pb3[piece(z, 16), :], rb3, b3)
    here_b = big_ref.at[core, 1, span(b_own + z * 16, 16)]
    b4 = [remote(here_b, here_b, z_peer(k)) for k in far]

    def four(ref):
        value = ref[0].astype(F32)
        for i in range(1, 4):
            value = value + ref[i].astype(F32)
        return value.astype(BF16)

    for copy in s2:
        copy.wait_recv()
    sy[y] = four(sx)
    s3 = [remote(sy.at[y], sy.at[y], y_peer(k)) for k in (2, 1, 3)]

    for copy in a4:
        copy.wait_recv()
    mid = big_ref.at[core, 0, span(a_own, 128)]
    a5 = [remote(mid, mid, y_peer(k)) for k in (2, 1, 3)]
    for copy in b4:
        copy.wait_recv()
    mid_b = big_ref.at[core, 1, span(b_own, 128)]
    b5 = [remote(mid_b, mid_b, x_peer(k)) for k in (2, 1, 3)]

    for copy in s3:
        copy.wait_recv()
    small_ref[core, piece(z, 48), :] = four(sy)
    bit = small_ref.at[core, piece(z, 48)]
    s4 = [remote(bit, bit, z_peer(k)) for k in far]

    for copy in a5:
        copy.wait_recv()
    quarter = big_ref.at[core, 0, piece(x, 512)]
    order = (2, 1, 3)
    a6 = [remote(quarter, quarter, x_peer(k)) for k in order]
    for copy in b5:
        copy.wait_recv()
    quarter_b = big_ref.at[core, 1, piece(y, 512)]
    b6 = [remote(quarter_b, quarter_b, y_peer(k)) for k in order]

    last = [remote(quarter, quarter, sibling), remote(quarter_b, quarter_b, sibling)]
    for copy in s4:
        copy.wait_recv()
    last.append(remote(small_ref.at[core], small_ref.at[core], sibling))
    for i in (1, 2, 0):
        k = order[i]
        a6[i].wait_recv()
        got = big_ref.at[core, 0, piece((x + 4 - k) % 4, 512)]
        last.append(remote(got, got, sibling))
        b6[i].wait_recv()
        got_b = big_ref.at[core, 1, piece((y + 4 - k) % 4, 512)]
        last.append(remote(got_b, got_b, sibling))
    for copy in last:
        copy.wait_recv()
    for copy in started:
        copy.wait_send()


N_SEM = 140


def widen(big_ref, small_ref, in_ref, out_ref, mix_ref):
    for j in range(4):
        in_ref[:, j * 128 : (j + 1) * 128] = big_ref[0, j // 2, j % 2].astype(F32)

    @pl.when((pl.program_id(0) == 0) & (pl.program_id(1) == 0))
    def _():
        for h in range(2):
            out_ref[h * 256 : (h + 1) * 256, :] = small_ref[h, 0:256].astype(F32)
            mix_ref[h * 128 : (h + 1) * 128, :] = small_ref[h, 256:384].astype(F32)


def on_device(patches, w_mix, w_in, w_out, partner_dev, partner_row):
    vmem = pltpu.VMEM
    any_spec = pl.BlockSpec(memory_space=pl.ANY)
    vmem_spec = pl.BlockSpec(memory_space=pltpu.VMEM)
    scratch = [
        vmem((COUNT * ANGLES, LANES), BF16),
        vmem((256, 512), BF16),
        vmem((LANES, FILTERS), BF16),
        vmem((FEATS, HIDDEN), BF16),
        vmem((HIDDEN, EMBED), BF16),
        vmem((2 * FREQS * COUNT, LANES), BF16),
        vmem((LANES, 2 * FREQS * COUNT), BF16),
        vmem((FREQS * COUNT, FILTERS), F32),
        vmem((FREQS * COUNT, FILTERS), F32),
        vmem((COUNT, FEATS), F32),
        vmem((COUNT, FEATS), BF16),
        vmem((COUNT, HIDDEN), F32),
        vmem((HIDDEN, COUNT), BF16),
        vmem((COUNT, FEATS), F32),
        vmem((2 * FREQS * COUNT, FILTERS), BF16),
        vmem((GROUP, EMBED), BF16),
        vmem((PEERS * SLOT, COUNT), F32),
        vmem((PEERS * SLOT, COUNT), F32),
        vmem((PEERS * SLOT, EMBED), F32),
        vmem((PEERS * SLOT, EMBED), F32),
        vmem((PEERS * SLOT, EMBED), F32),
        vmem((PEERS * SLOT, EMBED), F32),
        vmem((CYCLE * SLOT, COUNT), F32),
        vmem((FEATS // 2, COUNT), BF16),
        vmem((FEATS // 2, COUNT), BF16),
        vmem((FEATS // 2, COUNT), BF16),
        vmem((COUNT, HIDDEN), BF16),
        vmem((COUNT, HIDDEN), BF16),
        vmem((2048, 128), BF16),
        vmem((2048, 128), BF16),
        vmem((3, 512, 128), BF16),
        vmem((3, 512, 128), BF16),
        vmem((512, 128), BF16),
        vmem((512, 128), BF16),
        vmem((3, 128, 128), BF16),
        vmem((3, 128, 128), BF16),
        vmem((128, 128), BF16),
        vmem((128, 128), BF16),
        vmem((7, 16, 128), BF16),
        vmem((7, 16, 128), BF16),
        vmem((2, SMALL, 128), F32),
        vmem((SMALL, 128), F32),
        vmem((SMALL, 128), BF16),
        vmem((7, 48, 128), BF16),
        vmem((4, 48, 128), BF16),
        vmem((4, 48, 128), BF16),
        pltpu.SemaphoreType.DMA((12,)),
        pltpu.SemaphoreType.DMA((N_SEM,)),
        pltpu.SemaphoreType.DMA((N_SEM,)),
    ]
    loss, big, small = pl.pallas_call(
        kernel,
        name="contrastive_step",
        out_shape=(
            jax.ShapeDtypeStruct((1, COUNT), F32),
            jax.ShapeDtypeStruct((2, 2, 2048, 128), BF16),
            jax.ShapeDtypeStruct((2, SMALL, 128), BF16),
        ),
        in_specs=[vmem_spec, vmem_spec] + [any_spec] * 5,
        out_specs=(vmem_spec, vmem_spec, vmem_spec),
        scratch_shapes=scratch,
        compiler_params=pltpu.CompilerParams(
            collective_id=0, has_side_effects=True, vmem_limit_bytes=56 * 2**20
        ),
    )(
        partner_dev.reshape(1, COUNT),
        partner_row.reshape(1, COUNT),
        jnp.asarray(block_table()),
        w_mix,
        w_in,
        w_out,
        patches.reshape(COUNT * ANGLES, LANES),
    )
    rows = 256
    steps = FEATS // 2 // rows
    g_in, g_out, g_mix = pl.pallas_call(
        widen,
        name="widen",
        grid=(2, steps),
        out_shape=(
            jax.ShapeDtypeStruct((FEATS, HIDDEN), F32),
            jax.ShapeDtypeStruct((HIDDEN, EMBED), F32),
            jax.ShapeDtypeStruct((LANES, FILTERS), F32),
        ),
        in_specs=[
            pl.BlockSpec((1, 2, 2, rows, 128), lambda c, i: (c, 0, 0, i, 0)),
            pl.BlockSpec((2, SMALL, 128), lambda c, i: (0, 0, 0)),
        ],
        out_specs=(
            pl.BlockSpec((rows, HIDDEN), lambda c, i: (c * steps + i, 0)),
            pl.BlockSpec((HIDDEN, EMBED), lambda c, i: (0, 0)),
            pl.BlockSpec((LANES, FILTERS), lambda c, i: (0, 0)),
        ),
    )(big.reshape(2, 2, 2, FEATS // 2, 128), small)
    return (loss.reshape(COUNT), g_mix, g_in, g_out)


def solution(mesh):
    placed = (P(("blk", "dp"), None, None), P(), P(), P(), P(("blk", "dp")), P(("blk", "dp")))
    return jax.shard_map(
        on_device,
        mesh=mesh,
        in_specs=placed,
        out_specs=(P(("blk", "dp")), P(), P(), P()),
        check_vma=False,
    )
```

```python
import functools
import math

import jax
import jax.numpy as jnp
import ml_dtypes
import numpy as np
from jax import lax
from jax.experimental import pallas as pl
from jax.experimental.pallas import tpu as pltpu
from jax.sharding import PartitionSpec as P

SCALE = 10.0
MESH = pl.DeviceIdType.MESH
F32 = jnp.float32
BF16 = jnp.bfloat16

COUNT = 128
ANGLES = 64
LANES = 256
FREQS = 16
FILTERS = 128
FEATS = FREQS * FILTERS
HIDDEN = 512
EMBED = 128
PEERS = 32
CYCLE = 8
GROUP = CYCLE * COUNT
SLOT = COUNT // PEERS
TILE = 8
SMALL = 384
COEF = SCALE / COUNT


def block_table():
    angle = np.arange(ANGLES)
    freq = np.arange(FREQS)
    phase = np.mod(freq[None, :] * angle[:, None], ANGLES).astype(np.float32) * np.float32(
        2.0 * math.pi / ANGLES
    )
    table = np.concatenate([np.cos(phase), -np.sin(phase)], axis=1)
    wide = np.zeros((2 * FREQS, 8, 8, ANGLES), np.float32)
    for n in range(8):
        wide[:, n, n, :] = table.T
    return wide.reshape(2 * FREQS * 8, 8 * ANGLES).astype(ml_dtypes.bfloat16)


def dot(a, b):
    return jnp.dot(a, b, preferred_element_type=F32)


def dot_t(a, b):
    return lax.dot_general(a, b, (((1,), (1,)), ((), ())), preferred_element_type=F32)


def split(v):
    high = v.astype(BF16)
    return high, (v - high.astype(F32)).astype(BF16)


def iota(shape, dim):
    return lax.broadcasted_iota(jnp.int32, shape, dim)


def kernel(
    pdev_ref, prow_ref, table_hbm, wmix_hbm, win_hbm, wout_hbm, patches_hbm,
    loss_ref, big_ref, small_ref,
    patches, table, wmix, win, wout,
    spec, spec_t, real, imag, feat, normed, preact, hid_t, ngrad, mixg,
    group, ask_out, ask_in, row_out, row_in, back_out, back_in, tot_all,
    nt_own, nt_send, nt_sib, gp_own, gp_sib,
    pa, pb, ra1, rb1, pa2, pb2, ra2, rb2, pa3, pb3, ra3, rb3,
    sm, sm_sib, sm0, sz, sx, sy,
    big, small, loss,
    load_sem, keep_sem, send_sem, recv_sem,
):
    blk = lax.axis_index("blk")
    dp = lax.axis_index("dp")
    y = blk // 2
    x = (blk % 2) * 2 + dp // 16
    z = (dp // 2) % 8
    core = dp % 2
    other = 1 - core

    def device(x_, y_, z_, c_):
        return (y_ * 2 + x_ // 2, ((x_ % 2) * 8 + z_) * 2 + c_)

    sibling = device(x, y, z, other)

    def dp_peer(i):
        quad = i // 4
        half = (quad + 1) // 2
        dz = 4 + half * (2 * (quad % 2) - 1)
        xl = (dp // 16 + 1 - (i % 4) // 2) % 2
        c = (core + 1 - i % 2) % 2
        return (xl * 8 + (z + dz) % 8) * 2 + c

    used = [0]
    started = []

    def remote(src, dst, to):
        k = used[0]
        used[0] += 1
        copy = pltpu.make_async_remote_copy(
            src_ref=src, dst_ref=dst, send_sem=send_sem.at[k], recv_sem=recv_sem.at[k],
            device_id=to, device_id_type=MESH,
        )
        copy.start()
        started.append(copy)
        return copy

    def spread(value, src, dst):
        k = used[0]
        used[0] += 1
        for p in range(PEERS):
            src[p] = value[p * SLOT : (p + 1) * SLOT]

        def send(i, carry):
            p = dp_peer(i)
            pltpu.make_async_remote_copy(
                src_ref=src.at[p], dst_ref=dst.at[dp],
                send_sem=send_sem.at[k], recv_sem=recv_sem.at[k],
                device_id=(blk, p), device_id_type=MESH,
            ).start()
            return carry

        lax.fori_loop(0, PEERS - 1, send, 0)
        dst[dp] = src[dp]
        rows = pl.ds(0, PEERS - 1)
        whole = pltpu.make_async_remote_copy(
            src_ref=src.at[rows], dst_ref=dst.at[rows], send_sem=send_sem.at[k],
            recv_sem=recv_sem.at[k], device_id=(blk, dp_peer(0)), device_id_type=MESH,
        )
        started.append(whole)
        return whole

    def flat(ref):
        return jnp.concatenate([ref[p] for p in range(PEERS)], axis=0)

    def to_group(ref, rows):
        k = used[0]
        used[0] += 1
        mine = pl.ds(pl.multiple_of(blk * rows, rows), rows)
        for step in (5, 4, 3, 2, 1, 6, 7):
            pltpu.make_async_remote_copy(
                src_ref=ref.at[mine], dst_ref=ref.at[mine],
                send_sem=send_sem.at[k], recv_sem=recv_sem.at[k],
                device_id=((blk + step) % CYCLE, dp), device_id_type=MESH,
            ).start()
        span = pl.ds(0, (CYCLE - 1) * rows)
        whole = pltpu.make_async_remote_copy(
            src_ref=ref.at[span], dst_ref=ref.at[span], send_sem=send_sem.at[k],
            recv_sem=recv_sem.at[k], device_id=((blk + 1) % CYCLE, dp), device_id_type=MESH,
        )
        started.append(whole)
        return whole

    kept = []

    def keep(src, dst):
        copy = pltpu.make_async_copy(src, dst, keep_sem.at[len(kept)])
        copy.start()
        kept.append(copy)

    chunk = 1024
    loads = [pltpu.make_async_copy(table_hbm, table, load_sem.at[0])]
    for g in range(8):
        rows = pl.ds(g * chunk, chunk)
        loads.append(pltpu.make_async_copy(patches_hbm.at[rows], patches.at[rows], load_sem.at[1 + g]))
    loads.append(pltpu.make_async_copy(wmix_hbm, wmix, load_sem.at[9]))
    loads.append(pltpu.make_async_copy(win_hbm, win, load_sem.at[10]))
    loads.append(pltpu.make_async_copy(wout_hbm, wout, load_sem.at[11]))
    for load in loads:
        load.start()

    barrier = pltpu.get_barrier_semaphore()

    def greet(i, carry):
        pl.semaphore_signal(barrier, inc=1, device_id=(blk, dp_peer(i)), device_id_type=MESH)
        return carry

    lax.fori_loop(0, PEERS - 1, greet, 0)
    for step in range(1, CYCLE):
        pl.semaphore_signal(barrier, inc=1, device_id=((blk + step) % CYCLE, dp), device_id_type=MESH)
    pl.semaphore_signal(barrier, inc=1, device_id=device(3 - x, y, z, core), device_id_type=MESH)

    lane = iota((COUNT, COUNT), 1)
    row = iota((COUNT, COUNT), 0)
    dev_lane = jnp.broadcast_to(pdev_ref[...], (COUNT, COUNT))
    dev_row = dev_lane.astype(F32).T.astype(jnp.int32)
    same = dev_lane == dev_row
    rank_lane = jnp.sum(jnp.where(same & (row < lane), 1.0, 0.0), axis=0, keepdims=True)
    rank_row = jnp.sum(jnp.where(same & (lane < row), 1.0, 0.0), axis=1, keepdims=True)
    place_lane = pdev_ref[...] * SLOT + rank_lane.astype(jnp.int32)
    place_row = dev_row[:, :1] * SLOT + rank_row.astype(jnp.int32)
    to_slot = jnp.where(
        iota((PEERS * SLOT, COUNT), 0) == place_lane, 1.0, 0.0
    ).astype(BF16)
    from_slot = jnp.where(
        iota((COUNT, PEERS * SLOT), 1) == place_row, 1.0, 0.0
    ).astype(BF16)
    prow = jnp.broadcast_to(prow_ref[...], (COUNT, COUNT)).astype(F32).T.astype(BF16)
    ask = dot(to_slot, prow)

    loads[0].wait()
    bank = table[...]
    for g in range(8):
        loads[1 + g].wait()
        low = dot(bank, patches[g * chunk : g * chunk + 512, :])
        high = dot(bank, patches[g * chunk + 512 : (g + 1) * chunk, :])
        for k in range(2 * FREQS):
            part = jnp.concatenate([low[k * 8 : k * 8 + 8], high[k * 8 : k * 8 + 8]], axis=0)
            spec[k * COUNT + g * 16 : k * COUNT + g * 16 + 16, :] = part.astype(BF16)

    pl.semaphore_wait(barrier, PEERS - 1 + CYCLE - 1 + 1)
    asked = spread(ask, ask_out, ask_in)

    loads[9].wait()
    total = jnp.zeros((COUNT, 1), F32)
    for k in range(0, FREQS, 4):
        rows = slice(k * COUNT, (k + 4) * COUNT)
        re = dot(spec[rows, :], wmix[...])
        im = dot(spec[(FREQS + k) * COUNT : (FREQS + k + 4) * COUNT, :], wmix[...])
        real[rows, :] = re
        imag[rows, :] = im
        value = jnp.log1p(re * re + im * im)
        acc = jnp.zeros((COUNT, FILTERS), F32)
        for i in range(4):
            piece = value[i * COUNT : (i + 1) * COUNT]
            feat[:, (k + i) * FILTERS : (k + i + 1) * FILTERS] = piece
            acc = acc + piece
        total = total + jnp.sum(acc, axis=1, keepdims=True)
    mean = total * (1.0 / FEATS)
    acc = jnp.zeros((COUNT, FILTERS), F32)
    for k in range(FREQS):
        off = feat[:, k * FILTERS : (k + 1) * FILTERS] - mean
        acc = acc + off * off
    rscale = lax.rsqrt(jnp.sum(acc, axis=1, keepdims=True) * (1.0 / FEATS) + 1e-05)
    for k in range(FREQS):
        cols = slice(k * FILTERS, (k + 1) * FILTERS)
        hat = (feat[:, cols] - mean) * rscale
        feat[:, cols] = hat
        normed[:, cols] = hat.astype(BF16)

    loads[10].wait()
    pre = dot(normed[...], win[...])
    preact[...] = pre
    hidden = (pre * jax.nn.sigmoid(pre)).astype(BF16)
    loads[11].wait()
    raw = dot(hidden, wout[...])
    norms = jnp.sqrt(jnp.sum(raw * raw, axis=1, keepdims=True) + 1e-06)
    unit32 = raw / norms
    units = unit32.astype(BF16)
    group[pl.ds(pl.multiple_of(blk * COUNT, COUNT), COUNT), :] = units
    gathered = to_group(group, COUNT)

    asked.wait_recv()
    pick32 = jnp.where(flat(ask_in) == lane.astype(F32), 1.0, 0.0)
    returned = spread(dot(pick32.astype(BF16), units), row_out, row_in)

    unpick = pick32.T.astype(BF16)
    base = core * (FEATS // 2)
    for k in range(8):
        cols = pl.ds(pl.multiple_of((1 - core) * (FEATS // 2) + k * FILTERS, FILTERS), FILTERS)
        nt_send[k * FILTERS : (k + 1) * FILTERS, :] = normed[:, cols].T
    factor = remote(nt_send, nt_sib, sibling)
    for k in range(8):
        cols = pl.ds(pl.multiple_of(base + k * FILTERS, FILTERS), FILTERS)
        nt_own[k * FILTERS : (k + 1) * FILTERS, :] = normed[:, cols].T
    hid_t[...] = hidden.T
    for k in range(2 * FREQS):
        spec_t[:, k * COUNT : (k + 1) * COUNT] = spec[k * COUNT : (k + 1) * COUNT, :].T

    gathered.wait_recv()
    keys = group[...]
    scores = SCALE * dot_t(units, keys)
    self_lane = blk * COUNT + iota((COUNT, GROUP), 0)
    expo = jnp.where(iota((COUNT, GROUP), 1) == self_lane, 0.0, jnp.exp(scores))
    zneg = jnp.sum(expo, axis=1, keepdims=True)
    numer = dot(expo.astype(BF16), keys)

    returned.wait_recv()
    positive = dot(from_slot, flat(row_in).astype(BF16))
    own = units.astype(F32)
    spos = SCALE * jnp.sum(own * positive, axis=1, keepdims=True)
    epos = jnp.exp(spos)
    totals = epos + zneg
    tot_lane = jnp.broadcast_to(totals, (COUNT, COUNT)).T
    tot_all[pl.ds(pl.multiple_of(blk * TILE, TILE), TILE), :] = tot_lane[:TILE]
    tots = to_group(tot_all, TILE)
    away = COEF * (epos / totals - 1.0)
    high, low = split(away * own)
    backs = spread(dot(to_slot, high) + dot(to_slot, low), back_out, back_in)
    spos_lane = jnp.broadcast_to(spos, (COUNT, COUNT)).T
    loss[...] = (jnp.log(tot_lane) - spos_lane)[:1]
    keep(loss, loss_ref)
    grad_units = away * positive + COEF * (numer / totals)

    tots.wait_recv()
    inverse = jnp.concatenate(
        [1.0 / tot_all[b * TILE : b * TILE + 1, :] for b in range(CYCLE)], axis=1
    )
    keyterm = dot((expo * inverse).astype(BF16), keys)
    grad_units = grad_units + COEF * keyterm
    backs.wait_recv()
    high, low = split(flat(back_in))
    grad_units = grad_units + (dot(unpick, high) + dot(unpick, low))

    grad_raw = (
        (grad_units - unit32 * jnp.sum(unit32 * grad_units, axis=1, keepdims=True)) / norms
    ).astype(BF16)
    grad_hid = dot_t(grad_raw, wout[...])
    pre = preact[...]
    sigm = jax.nn.sigmoid(pre)
    grad_pre = (grad_hid * sigm * (1.0 + pre * (1.0 - sigm))).astype(BF16)
    gp_own[...] = grad_pre
    sent = remote(gp_own, gp_sib, sibling)
    g_out = dot(hid_t[...], grad_raw)
    sm[0, 0:256, :] = g_out[:256]
    sm[1, 0:256, :] = g_out[256:]
    ngrad[...] = dot_t(grad_pre, win[...])

    factor.wait_recv()
    sent.wait_recv()
    right = jnp.concatenate([gp_own[...], gp_sib[...]], axis=0)
    for i in range(4):
        rows = slice(i * 256, (i + 1) * 256)
        prod = dot(jnp.concatenate([nt_own[rows, :], nt_sib[rows, :]], axis=1), right)
        to = pa if i < 2 else pb
        to[(i % 2) * 256 : (i % 2 + 1) * 256, :] = prod.astype(BF16)

    def x_peer(k):
        return device((x + k) % 4, y, z, core)

    def y_peer(k):
        return device(x, (y + k) % 4, z, core)

    def z_peer(k):
        return device(x, y, (z + k) % 8, core)

    def piece(at, rows):
        return pl.ds(pl.multiple_of(at * rows, rows), rows)

    def cell(at):
        return (piece(at // 4, 16), piece(at % 4, 128))

    parts = (
        (pa, ra1, pa2, ra2, pa3, ra3, x, y, x_peer, y_peer),
        (pb, rb1, pb2, rb2, pb3, rb3, y, x, y_peer, x_peer),
    )
    far4 = (2, 1, 3)
    far = (4, 3, 5, 2, 6, 1, 7)
    step1 = ({}, {})
    for j in (2, 1, 3, 0):
        for n, (src, got, _, _, _, _, u, v, u_peer, _) in enumerate(parts):
            for k in far4:
                step1[n][j, k] = remote(
                    src.at[piece((u + k) % 4 * 4 + (v + j) % 4, 32)],
                    got.at[k - 1, piece((v + j) % 4, 32)],
                    u_peer(k),
                )

    acc = jnp.zeros((COUNT, FILTERS), F32)
    acc_hat = jnp.zeros((COUNT, FILTERS), F32)
    for k in range(FREQS):
        cols = slice(k * FILTERS, (k + 1) * FILTERS)
        ng = ngrad[:, cols]
        acc = acc + ng
        acc_hat = acc_hat + ng * feat[:, cols]
    mean_ng = jnp.sum(acc, axis=1, keepdims=True) * (1.0 / FEATS)
    mean_hat = jnp.sum(acc_hat, axis=1, keepdims=True) * (1.0 / FEATS)
    for k in range(FREQS):
        cols = slice(k * FILTERS, (k + 1) * FILTERS)
        rows = slice(k * COUNT, (k + 1) * COUNT)
        re = real[rows, :]
        im = imag[rows, :]
        grad_feat = rscale * (ngrad[:, cols] - mean_ng - feat[:, cols] * mean_hat)
        grad_pow = 2.0 * grad_feat / (1.0 + (re * re + im * im))
        mixg[rows, :] = (re * grad_pow).astype(BF16)
        mixg[(FREQS + k) * COUNT : (FREQS + k + 1) * COUNT, :] = (im * grad_pow).astype(BF16)
    g_mix = dot(spec_t[...], mixg[...])
    sm[0, 256:384, :] = g_mix[:128]
    sm[1, 256:384, :] = g_mix[128:]
    halves = remote(sm.at[other], sm_sib, sibling)

    def add(own_part, got, copies):
        value = own_part.astype(F32)
        for k in sorted(copies):
            copies[k].wait_recv()
            value = value + got[k - 1].astype(F32)
        return value.astype(BF16)

    step2 = ({}, {})
    for j in (2, 1, 3, 0):
        for n, (src, got, src2, got2, _, _, u, v, _, v_peer) in enumerate(parts):
            mine = piece((v + j) % 4, 32)
            value = src[piece(u * 4 + (v + j) % 4, 32), :].astype(F32)
            for k in (1, 3, 2):
                step1[n][j, k].wait_recv()
                value = value + got[k - 1, mine, :].astype(F32)
            src2[mine, :] = value.astype(BF16)
            if j:
                step2[n][j] = remote(src2.at[mine], got2.at[j - 1], v_peer(j))

    halves.wait_recv()
    sm0[...] = (sm[core] + sm_sib[...]).astype(BF16)
    s1 = {k: remote(sm0.at[piece((z + k) % 8, 48)], sz.at[k - 1], z_peer(k)) for k in far}

    step3 = ({}, {})
    for n, (_, _, src2, got2, src3, got3, _, v, _, _) in enumerate(parts):
        src3[...] = add(src2[piece(v, 32), :], got2, step2[n])
        for k in far:
            step3[n][k] = remote(src3.at[cell((z + k) % 8)], got3.at[k - 1], z_peer(k))

    sx[x] = add(sm0[piece(z, 48), :], sz, s1)
    s2 = [remote(sx.at[x], sx.at[x], x_peer(k)) for k in far4]

    def place(c, n, u, v, rows):
        return pl.ds(pl.multiple_of(c * 1024 + n * 512 + u * 128 + v * 32, 32), rows)

    step4 = ([], [])
    for n, (_, _, _, _, src3, got3, u, v, _, _) in enumerate(parts):
        block = big.at[place(core, n, u, v, 32)]
        block[cell(z)] = add(src3[cell(z)], got3, step3[n])
        for k in far:
            here = block.at[cell(z)]
            step4[n].append(remote(here, here, z_peer(k)))

    def four(ref):
        value = ref[0].astype(F32)
        for i in range(1, 4):
            value = value + ref[i].astype(F32)
        return value.astype(BF16)

    for copy in s2:
        copy.wait_recv()
    sy[y] = four(sx)
    s3 = [remote(sy.at[y], sy.at[y], y_peer(k)) for k in far4]

    step5 = ({}, {})
    step6 = ({}, {})

    def forward(n, m):
        u, v, u_peer = parts[n][6], parts[n][7], parts[n][8]
        block = big.at[place(core, n, u, (v + 4 - m) % 4, 32)]
        for k in far4:
            step6[n][m, k] = remote(block, block, u_peer(k))

    for n in range(2):
        u, v, v_peer = parts[n][6], parts[n][7], parts[n][9]
        for copy in step4[n]:
            copy.wait_recv()
        block = big.at[place(core, n, u, v, 32)]
        for k in far4:
            step5[n][k] = remote(block, block, v_peer(k))
        forward(n, 0)

    for copy in s3:
        copy.wait_recv()
    small[core, piece(z, 48), :] = four(sy)
    bit = small.at[core, piece(z, 48)]
    s4 = [remote(bit, bit, z_peer(k)) for k in far]

    for m in (1, 3, 2):
        for n in range(2):
            step5[n][m].wait_recv()
            forward(n, m)

    last = []

    def cross(n, u):
        chunk = place(core, n, u, 0, 128)
        last.append((remote(big.at[chunk], big.at[chunk], sibling), place(other, n, u, 0, 128)))
        keep(big.at[chunk], big_ref.at[chunk])

    for n in range(2):
        cross(n, parts[n][6])
    for copy in s4:
        copy.wait_recv()
    bits = remote(small.at[core], small.at[core], sibling)
    keep(small.at[core], small_ref.at[core])
    for k in (1, 3, 2):
        for n in range(2):
            for m in (0, 1, 3, 2):
                step6[n][m, k].wait_recv()
            cross(n, (parts[n][6] + 4 - k) % 4)
    bits.wait_recv()
    keep(small.at[other], small_ref.at[other])
    for copy, chunk in last:
        copy.wait_recv()
        keep(big.at[chunk], big_ref.at[chunk])
    for copy in started:
        copy.wait_send()
    for copy in kept:
        copy.wait()


N_SEM = 160
N_KEEP = 24


STEPS = 8


def widen(big_ref, small_ref, loss_ref, in_ref, out_ref, mix_ref, rows_ref, big, wide, small, small32, load_sem, store_sem):
    size = FEATS // STEPS
    loads = []
    stores = [pltpu.make_async_copy(loss_ref, rows_ref, store_sem.at[STEPS])]
    stores[0].start()
    for i in range(STEPS):
        rows = pl.ds(i * size, size)
        loads.append(pltpu.make_async_copy(big_ref.at[rows], big.at[rows], load_sem.at[i]))
    loads.append(pltpu.make_async_copy(small_ref, small, load_sem.at[STEPS]))
    for load in loads:
        load.start()
    for i in range(STEPS):
        rows = pl.ds(i * size, size)
        loads[i].wait()
        wide[rows, :] = big[rows, :].astype(F32)
        stores.append(pltpu.make_async_copy(wide.at[rows], in_ref.at[rows], store_sem.at[i]))
        stores[-1].start()
    loads[STEPS].wait()
    small32[...] = small[...].astype(F32)
    for h in range(2):
        at = small32.at[h, pl.ds(0, 256)]
        stores.append(pltpu.make_async_copy(at, out_ref.at[pl.ds(h * 256, 256)], store_sem.at[STEPS + 1 + h]))
        stores[-1].start()
        at = small32.at[h, pl.ds(256, 128)]
        stores.append(pltpu.make_async_copy(at, mix_ref.at[pl.ds(h * 128, 128)], store_sem.at[STEPS + 3 + h]))
        stores[-1].start()
    for store in stores:
        store.wait()


def on_device(patches, w_mix, w_in, w_out, partner_dev, partner_row):
    vmem = pltpu.VMEM
    any_spec = pl.BlockSpec(memory_space=pl.ANY)
    vmem_spec = pl.BlockSpec(memory_space=pltpu.VMEM)
    scratch = [
        vmem((COUNT * ANGLES, LANES), BF16),
        vmem((256, 512), BF16),
        vmem((LANES, FILTERS), BF16),
        vmem((FEATS, HIDDEN), BF16),
        vmem((HIDDEN, EMBED), BF16),
        vmem((2 * FREQS * COUNT, LANES), BF16),
        vmem((LANES, 2 * FREQS * COUNT), BF16),
        vmem((FREQS * COUNT, FILTERS), F32),
        vmem((FREQS * COUNT, FILTERS), F32),
        vmem((COUNT, FEATS), F32),
        vmem((COUNT, FEATS), BF16),
        vmem((COUNT, HIDDEN), F32),
        vmem((HIDDEN, COUNT), BF16),
        vmem((COUNT, FEATS), F32),
        vmem((2 * FREQS * COUNT, FILTERS), BF16),
        vmem((GROUP, EMBED), BF16),
        vmem((PEERS, SLOT, COUNT), F32),
        vmem((PEERS, SLOT, COUNT), F32),
        vmem((PEERS, SLOT, COUNT), F32),
        vmem((PEERS, SLOT, COUNT), F32),
        vmem((PEERS, SLOT, COUNT), F32),
        vmem((PEERS, SLOT, COUNT), F32),
        vmem((CYCLE * TILE, COUNT), F32),
        vmem((FEATS // 2, COUNT), BF16),
        vmem((FEATS // 2, COUNT), BF16),
        vmem((FEATS // 2, COUNT), BF16),
        vmem((COUNT, HIDDEN), BF16),
        vmem((COUNT, HIDDEN), BF16),
        vmem((512, 512), BF16),
        vmem((512, 512), BF16),
        vmem((3, 128, 512), BF16),
        vmem((3, 128, 512), BF16),
        vmem((128, 512), BF16),
        vmem((128, 512), BF16),
        vmem((3, 32, 512), BF16),
        vmem((3, 32, 512), BF16),
        vmem((32, 512), BF16),
        vmem((32, 512), BF16),
        vmem((7, 16, 128), BF16),
        vmem((7, 16, 128), BF16),
        vmem((2, SMALL, 128), F32),
        vmem((SMALL, 128), F32),
        vmem((SMALL, 128), BF16),
        vmem((7, 48, 128), BF16),
        vmem((4, 48, 128), BF16),
        vmem((4, 48, 128), BF16),
        vmem((FEATS, HIDDEN), BF16),
        vmem((2, SMALL, 128), BF16),
        vmem((1, COUNT), F32),
        pltpu.SemaphoreType.DMA((12,)),
        pltpu.SemaphoreType.DMA((N_KEEP,)),
        pltpu.SemaphoreType.DMA((N_SEM,)),
        pltpu.SemaphoreType.DMA((N_SEM,)),
    ]
    loss, big, small = pl.pallas_call(
        kernel,
        name="contrastive_step",
        out_shape=(
            jax.ShapeDtypeStruct((1, COUNT), F32),
            jax.ShapeDtypeStruct((FEATS, HIDDEN), BF16),
            jax.ShapeDtypeStruct((2, SMALL, 128), BF16),
        ),
        in_specs=[vmem_spec, vmem_spec] + [any_spec] * 5,
        out_specs=(any_spec, any_spec, any_spec),
        scratch_shapes=scratch,
        compiler_params=pltpu.CompilerParams(
            collective_id=0, has_side_effects=True, vmem_limit_bytes=56 * 2**20
        ),
    )(
        partner_dev.reshape(1, COUNT),
        partner_row.reshape(1, COUNT),
        jnp.asarray(block_table()),
        w_mix,
        w_in,
        w_out,
        patches.reshape(COUNT * ANGLES, LANES),
    )
    g_in, g_out, g_mix, loss = pl.pallas_call(
        widen,
        name="widen",
        out_shape=(
            jax.ShapeDtypeStruct((FEATS, HIDDEN), F32),
            jax.ShapeDtypeStruct((HIDDEN, EMBED), F32),
            jax.ShapeDtypeStruct((LANES, FILTERS), F32),
            jax.ShapeDtypeStruct((1, COUNT), F32),
        ),
        in_specs=[any_spec] * 3,
        out_specs=(any_spec,) * 4,
        scratch_shapes=[
            vmem((FEATS, HIDDEN), BF16),
            vmem((FEATS, HIDDEN), F32),
            vmem((2, SMALL, 128), BF16),
            vmem((2, SMALL, 128), F32),
            pltpu.SemaphoreType.DMA((STEPS + 1,)),
            pltpu.SemaphoreType.DMA((STEPS + 5,)),
        ],
        compiler_params=pltpu.CompilerParams(vmem_limit_bytes=56 * 2**20),
    )(big, small, loss)
    return (loss.reshape(COUNT), g_mix, g_in, g_out)


def solution(mesh):
    placed = (P(("blk", "dp"), None, None), P(), P(), P(), P(("blk", "dp")), P(("blk", "dp")))
    return jax.shard_map(
        on_device,
        mesh=mesh,
        in_specs=placed,
        out_specs=(P(("blk", "dp")), P(), P(), P()),
        check_vma=False,
    )
```

```python
import functools
import math

import jax
import jax.numpy as jnp
import ml_dtypes
import numpy as np
from jax import lax
from jax.experimental import pallas as pl
from jax.experimental.pallas import tpu as pltpu
from jax.sharding import PartitionSpec as P

SCALE = 10.0
MESH = pl.DeviceIdType.MESH
F32 = jnp.float32
BF16 = jnp.bfloat16

COUNT = 128
ANGLES = 64
LANES = 256
FREQS = 16
FILTERS = 128
FEATS = FREQS * FILTERS
HIDDEN = 512
EMBED = 128
PEERS = 32
CYCLE = 8
GROUP = CYCLE * COUNT
SLOT = COUNT // PEERS
TILE = 8
SMALL = 384
COEF = SCALE / COUNT


def block_table():
    angle = np.arange(ANGLES)
    freq = np.arange(FREQS)
    phase = np.mod(freq[None, :] * angle[:, None], ANGLES).astype(np.float32) * np.float32(
        2.0 * math.pi / ANGLES
    )
    table = np.concatenate([np.cos(phase), -np.sin(phase)], axis=1)
    wide = np.zeros((2 * FREQS, 8, 8, ANGLES), np.float32)
    for n in range(8):
        wide[:, n, n, :] = table.T
    return wide.reshape(2 * FREQS * 8, 8 * ANGLES).astype(ml_dtypes.bfloat16)


def dot(a, b):
    return jnp.dot(a, b, preferred_element_type=F32)


def dot_t(a, b):
    return lax.dot_general(a, b, (((1,), (1,)), ((), ())), preferred_element_type=F32)


def split(v):
    high = v.astype(BF16)
    return high, (v - high.astype(F32)).astype(BF16)


def iota(shape, dim):
    return lax.broadcasted_iota(jnp.int32, shape, dim)


def kernel(
    pdev_hbm, prow_hbm, table_hbm, wmix_hbm, win_hbm, wout_hbm, patches_hbm,
    loss_ref, big_ref, small_ref,
    pdev_ref, prow_ref, patches, table, wmix, win, wout,
    spec, spec_t, real, imag, feat, normed, preact, hid_t, ngrad, mixg,
    group, ask_out, ask_in, row_out, row_in, back_out, back_in, tot_all,
    nt_own, nt_send, nt_sib, gp_own, gp_sib,
    pa, pb, ra1, rb1, pa2, pb2, ra2, rb2, pa3, pb3, ra3, rb3,
    sm, sm_sib, sm0, sz, sx, sy,
    big, small, loss,
    load_sem, keep_sem, send_sem, recv_sem,
):
    blk = lax.axis_index("blk")
    dp = lax.axis_index("dp")
    y = lax.div(blk, 2)
    x_low = lax.div(dp, 16)
    x = lax.rem(blk, 2) * 2 + x_low
    z = lax.rem(lax.div(dp, 2), 8)
    core = lax.rem(dp, 2)
    other = 1 - core

    def device(x_, y_, z_, c_):
        return (y_ * 2 + lax.div(x_, 2), lax.rem(x_, 2) * 16 + z_ * 2 + c_)

    sibling = device(x, y, z, other)

    dp_peers = []
    for dz in (4, 5, 3, 6, 2, 7, 1, 0):
        z_part = lax.rem(z + dz, 8) * 2
        for x_part in ((1 - x_low) * 16, x_low * 16):
            for c_part in (other, core):
                dp_peers.append(x_part + z_part + c_part)
    dp_peers = dp_peers[:-1]
    blk_peers = [lax.rem(blk + step, CYCLE) for step in (5, 4, 3, 2, 1, 6, 7)]

    used = [0]
    started = []

    def remote(src, dst, to):
        k = used[0]
        used[0] += 1
        copy = pltpu.make_async_remote_copy(
            src_ref=src, dst_ref=dst, send_sem=send_sem.at[k], recv_sem=recv_sem.at[k],
            device_id=to, device_id_type=MESH,
        )
        copy.start()
        started.append(copy)
        return copy

    def spread(value, src, dst):
        k = used[0]
        used[0] += 1
        for p in range(PEERS):
            src[p] = value[p * SLOT : (p + 1) * SLOT]

        for p in dp_peers:
            pltpu.make_async_remote_copy(
                src_ref=src.at[p], dst_ref=dst.at[dp],
                send_sem=send_sem.at[k], recv_sem=recv_sem.at[k],
                device_id=(blk, p), device_id_type=MESH,
            ).start()
        dst[dp] = src[dp]
        rows = pl.ds(0, PEERS - 1)
        whole = pltpu.make_async_remote_copy(
            src_ref=src.at[rows], dst_ref=dst.at[rows], send_sem=send_sem.at[k],
            recv_sem=recv_sem.at[k], device_id=(blk, dp_peers[0]), device_id_type=MESH,
        )
        started.append(whole)
        return whole

    def flat(ref):
        return jnp.concatenate([ref[p] for p in range(PEERS)], axis=0)

    def to_group(ref, rows):
        k = used[0]
        used[0] += 1
        mine = pl.ds(pl.multiple_of(blk * rows, rows), rows)
        for b in blk_peers:
            pltpu.make_async_remote_copy(
                src_ref=ref.at[mine], dst_ref=ref.at[mine],
                send_sem=send_sem.at[k], recv_sem=recv_sem.at[k],
                device_id=(b, dp), device_id_type=MESH,
            ).start()
        span = pl.ds(0, (CYCLE - 1) * rows)
        whole = pltpu.make_async_remote_copy(
            src_ref=ref.at[span], dst_ref=ref.at[span], send_sem=send_sem.at[k],
            recv_sem=recv_sem.at[k], device_id=(blk_peers[0], dp), device_id_type=MESH,
        )
        started.append(whole)
        return whole

    kept = []

    def keep(src, dst):
        copy = pltpu.make_async_copy(src, dst, keep_sem.at[len(kept)])
        copy.start()
        kept.append(copy)

    barrier = pltpu.get_barrier_semaphore()

    for p in dp_peers:
        pl.semaphore_signal(barrier, inc=1, device_id=(blk, p), device_id_type=MESH)
    for b in blk_peers:
        pl.semaphore_signal(barrier, inc=1, device_id=(b, dp), device_id_type=MESH)
    pl.semaphore_signal(barrier, inc=1, device_id=device(3 - x, y, z, core), device_id_type=MESH)

    chunk = 1024
    loads = [pltpu.make_async_copy(table_hbm, table, load_sem.at[0])]
    for g in range(8):
        rows = pl.ds(g * chunk, chunk)
        loads.append(pltpu.make_async_copy(patches_hbm.at[rows], patches.at[rows], load_sem.at[1 + g]))
    loads.append(pltpu.make_async_copy(wmix_hbm, wmix, load_sem.at[9]))
    loads.append(pltpu.make_async_copy(win_hbm, win, load_sem.at[10]))
    loads.append(pltpu.make_async_copy(wout_hbm, wout, load_sem.at[11]))
    loads.append(pltpu.make_async_copy(pdev_hbm, pdev_ref, load_sem.at[12]))
    loads.append(pltpu.make_async_copy(prow_hbm, prow_ref, load_sem.at[13]))
    for i in (12, 13) + tuple(range(12)):
        loads[i].start()

    loads[12].wait()
    loads[13].wait()
    lane = iota((COUNT, COUNT), 1)
    row = iota((COUNT, COUNT), 0)
    dev_lane = jnp.broadcast_to(pdev_ref[...], (COUNT, COUNT))
    dev_row = dev_lane.astype(F32).T.astype(jnp.int32)
    same = dev_lane == dev_row
    rank_lane = jnp.sum(jnp.where(same & (row < lane), 1.0, 0.0), axis=0, keepdims=True)
    rank_row = jnp.sum(jnp.where(same & (lane < row), 1.0, 0.0), axis=1, keepdims=True)
    place_lane = pdev_ref[...] * SLOT + rank_lane.astype(jnp.int32)
    place_row = dev_row[:, :1] * SLOT + rank_row.astype(jnp.int32)
    to_slot = jnp.where(
        iota((PEERS * SLOT, COUNT), 0) == place_lane, 1.0, 0.0
    ).astype(BF16)
    from_slot = jnp.where(
        iota((COUNT, PEERS * SLOT), 1) == place_row, 1.0, 0.0
    ).astype(BF16)
    prow = jnp.broadcast_to(prow_ref[...], (COUNT, COUNT)).astype(F32).T.astype(BF16)
    ask = dot(to_slot, prow)

    loads[0].wait()
    bank = table[...]
    for g in range(8):
        loads[1 + g].wait()
        low = dot(bank, patches[g * chunk : g * chunk + 512, :])
        high = dot(bank, patches[g * chunk + 512 : (g + 1) * chunk, :])
        for k in range(2 * FREQS):
            part = jnp.concatenate([low[k * 8 : k * 8 + 8], high[k * 8 : k * 8 + 8]], axis=0)
            spec[k * COUNT + g * 16 : k * COUNT + g * 16 + 16, :] = part.astype(BF16)
        if g == 2:
            pl.semaphore_wait(barrier, PEERS - 1 + CYCLE - 1 + 1)
            asked = spread(ask, ask_out, ask_in)

    loads[9].wait()
    total = jnp.zeros((COUNT, 1), F32)
    for k in range(0, FREQS, 4):
        rows = slice(k * COUNT, (k + 4) * COUNT)
        re = dot(spec[rows, :], wmix[...])
        im = dot(spec[(FREQS + k) * COUNT : (FREQS + k + 4) * COUNT, :], wmix[...])
        real[rows, :] = re
        imag[rows, :] = im
        value = jnp.log1p(re * re + im * im)
        acc = jnp.zeros((COUNT, FILTERS), F32)
        for i in range(4):
            piece = value[i * COUNT : (i + 1) * COUNT]
            feat[:, (k + i) * FILTERS : (k + i + 1) * FILTERS] = piece
            acc = acc + piece
        total = total + jnp.sum(acc, axis=1, keepdims=True)
    mean = total * (1.0 / FEATS)
    acc = jnp.zeros((COUNT, FILTERS), F32)
    for k in range(FREQS):
        off = feat[:, k * FILTERS : (k + 1) * FILTERS] - mean
        acc = acc + off * off
    rscale = lax.rsqrt(jnp.sum(acc, axis=1, keepdims=True) * (1.0 / FEATS) + 1e-05)
    for k in range(FREQS):
        cols = slice(k * FILTERS, (k + 1) * FILTERS)
        hat = (feat[:, cols] - mean) * rscale
        feat[:, cols] = hat
        normed[:, cols] = hat.astype(BF16)

    loads[10].wait()
    pre = dot(normed[...], win[...])
    preact[...] = pre
    hidden = (pre * jax.nn.sigmoid(pre)).astype(BF16)
    loads[11].wait()
    raw = dot(hidden, wout[...])
    norms = jnp.sqrt(jnp.sum(raw * raw, axis=1, keepdims=True) + 1e-06)
    unit32 = raw / norms
    units = unit32.astype(BF16)
    group[pl.ds(pl.multiple_of(blk * COUNT, COUNT), COUNT), :] = units
    gathered = to_group(group, COUNT)

    asked.wait_recv()
    pick32 = jnp.where(flat(ask_in) == lane.astype(F32), 1.0, 0.0)
    returned = spread(dot(pick32.astype(BF16), units), row_out, row_in)

    unpick = pick32.T.astype(BF16)
    base = core * (FEATS // 2)
    for k in range(8):
        cols = pl.ds(pl.multiple_of((1 - core) * (FEATS // 2) + k * FILTERS, FILTERS), FILTERS)
        nt_send[k * FILTERS : (k + 1) * FILTERS, :] = normed[:, cols].T
    factor = remote(nt_send, nt_sib, sibling)
    for k in range(8):
        cols = pl.ds(pl.multiple_of(base + k * FILTERS, FILTERS), FILTERS)
        nt_own[k * FILTERS : (k + 1) * FILTERS, :] = normed[:, cols].T

    gathered.wait_recv()
    keys = group[...]
    scores = SCALE * dot_t(units, keys)
    self_lane = blk * COUNT + iota((COUNT, GROUP), 0)
    expo = jnp.where(iota((COUNT, GROUP), 1) == self_lane, 0.0, jnp.exp(scores))
    zneg = jnp.sum(expo, axis=1, keepdims=True)
    numer = dot(expo.astype(BF16), keys)

    returned.wait_recv()
    positive = dot(from_slot, flat(row_in).astype(BF16))
    own = units.astype(F32)
    spos = SCALE * jnp.sum(own * positive, axis=1, keepdims=True)
    epos = jnp.exp(spos)
    totals = epos + zneg
    tot_lane = jnp.broadcast_to(totals, (COUNT, COUNT)).T
    tot_all[pl.ds(pl.multiple_of(blk * TILE, TILE), TILE), :] = tot_lane[:TILE]
    tots = to_group(tot_all, TILE)
    away = COEF * (epos / totals - 1.0)
    high, low = split(away * own)
    backs = spread(dot(to_slot, high) + dot(to_slot, low), back_out, back_in)
    spos_lane = jnp.broadcast_to(spos, (COUNT, COUNT)).T
    loss[...] = (jnp.log(tot_lane) - spos_lane)[:1]
    keep(loss, loss_ref)
    grad_units = away * positive + COEF * (numer / totals)
    hid_t[...] = hidden.T
    for k in range(2 * FREQS):
        spec_t[:, k * COUNT : (k + 1) * COUNT] = spec[k * COUNT : (k + 1) * COUNT, :].T

    tots.wait_recv()
    inverse = jnp.concatenate(
        [1.0 / tot_all[b * TILE : b * TILE + 1, :] for b in range(CYCLE)], axis=1
    )
    keyterm = dot((expo * inverse).astype(BF16), keys)
    grad_units = grad_units + COEF * keyterm
    backs.wait_recv()
    high, low = split(flat(back_in))
    grad_units = grad_units + (dot(unpick, high) + dot(unpick, low))

    grad_raw = (
        (grad_units - unit32 * jnp.sum(unit32 * grad_units, axis=1, keepdims=True)) / norms
    ).astype(BF16)
    grad_hid = dot_t(grad_raw, wout[...])
    pre = preact[...]
    sigm = jax.nn.sigmoid(pre)
    grad_pre = (grad_hid * sigm * (1.0 + pre * (1.0 - sigm))).astype(BF16)
    gp_own[...] = grad_pre
    sent = remote(gp_own, gp_sib, sibling)
    g_out = dot(hid_t[...], grad_raw)
    sm[0, 0:256, :] = g_out[:256]
    sm[1, 0:256, :] = g_out[256:]
    ngrad[...] = dot_t(grad_pre, win[...])

    factor.wait_recv()
    sent.wait_recv()
    right = jnp.concatenate([gp_own[...], gp_sib[...]], axis=0)
    for i in range(4):
        rows = slice(i * 256, (i + 1) * 256)
        prod = dot(jnp.concatenate([nt_own[rows, :], nt_sib[rows, :]], axis=1), right)
        to = pa if i < 2 else pb
        to[(i % 2) * 256 : (i % 2 + 1) * 256, :] = prod.astype(BF16)

    xs = [lax.rem(x + k, 4) for k in range(4)]
    ys = [lax.rem(y + k, 4) for k in range(4)]
    zs = [lax.rem(z + k, 8) for k in range(8)]
    x_peers = [device(xs[k], y, z, core) for k in range(4)]
    y_peers = [device(x, ys[k], z, core) for k in range(4)]
    z_peers = [device(x, y, zs[k], core) for k in range(8)]

    def piece(at, rows):
        return pl.ds(pl.multiple_of(at * rows, rows), rows)

    def cell(at):
        return (piece(lax.div(at, 4), 16), piece(lax.rem(at, 4), 128))

    parts = (
        (pa, ra1, pa2, ra2, pa3, ra3, xs, ys, x_peers, y_peers),
        (pb, rb1, pb2, rb2, pb3, rb3, ys, xs, y_peers, x_peers),
    )
    far4 = (2, 1, 3)
    far = (4, 3, 5, 2, 6, 1, 7)
    step1 = ({}, {})
    for j in (2, 1, 3, 0):
        for n, (src, got, _, _, _, _, u, v, u_peer, _) in enumerate(parts):
            for k in far4:
                step1[n][j, k] = remote(
                    src.at[piece(u[k] * 4 + v[j], 32)],
                    got.at[k - 1, piece(v[j], 32)],
                    u_peer[k],
                )

    acc = jnp.zeros((COUNT, FILTERS), F32)
    acc_hat = jnp.zeros((COUNT, FILTERS), F32)
    for k in range(FREQS):
        cols = slice(k * FILTERS, (k + 1) * FILTERS)
        ng = ngrad[:, cols]
        acc = acc + ng
        acc_hat = acc_hat + ng * feat[:, cols]
    mean_ng = jnp.sum(acc, axis=1, keepdims=True) * (1.0 / FEATS)
    mean_hat = jnp.sum(acc_hat, axis=1, keepdims=True) * (1.0 / FEATS)
    for k in range(FREQS):
        cols = slice(k * FILTERS, (k + 1) * FILTERS)
        rows = slice(k * COUNT, (k + 1) * COUNT)
        re = real[rows, :]
        im = imag[rows, :]
        grad_feat = rscale * (ngrad[:, cols] - mean_ng - feat[:, cols] * mean_hat)
        grad_pow = 2.0 * grad_feat / (1.0 + (re * re + im * im))
        mixg[rows, :] = (re * grad_pow).astype(BF16)
        mixg[(FREQS + k) * COUNT : (FREQS + k + 1) * COUNT, :] = (im * grad_pow).astype(BF16)
    g_mix = dot(spec_t[...], mixg[...])
    sm[0, 256:384, :] = g_mix[:128]
    sm[1, 256:384, :] = g_mix[128:]
    halves = remote(sm.at[other], sm_sib, sibling)

    def add(own_part, got, copies):
        value = own_part.astype(F32)
        for k in sorted(copies):
            copies[k].wait_recv()
            value = value + got[k - 1].astype(F32)
        return value.astype(BF16)

    step2 = ({}, {})
    for j in (2, 1, 3, 0):
        for n, (src, got, src2, got2, _, _, u, v, _, v_peer) in enumerate(parts):
            mine = piece(v[j], 32)
            value = src[piece(u[0] * 4 + v[j], 32), :].astype(F32)
            for k in (1, 3, 2):
                step1[n][j, k].wait_recv()
                value = value + got[k - 1, mine, :].astype(F32)
            src2[mine, :] = value.astype(BF16)
            if j:
                step2[n][j] = remote(src2.at[mine], got2.at[j - 1], v_peer[j])

    halves.wait_recv()
    sm0[...] = (sm[core] + sm_sib[...]).astype(BF16)
    s1 = {k: remote(sm0.at[piece(zs[k], 48)], sz.at[k - 1], z_peers[k]) for k in far}

    step3 = ({}, {})
    for n, (_, _, src2, got2, src3, got3, _, v, _, _) in enumerate(parts):
        src3[...] = add(src2[piece(v[0], 32), :], got2, step2[n])
        for k in far:
            step3[n][k] = remote(src3.at[cell(zs[k])], got3.at[k - 1], z_peers[k])

    sx[x] = add(sm0[piece(z, 48), :], sz, s1)
    s2 = [remote(sx.at[x], sx.at[x], x_peers[k]) for k in far4]

    def place(c, n, u, v, rows):
        return pl.ds(pl.multiple_of(c * 1024 + n * 512 + u * 128 + v * 32, 32), rows)

    step4 = ([], [])
    for n, (_, _, _, _, src3, got3, u, v, _, _) in enumerate(parts):
        block = big.at[place(core, n, u[0], v[0], 32)]
        block[cell(z)] = add(src3[cell(z)], got3, step3[n])
        for k in far:
            here = block.at[cell(z)]
            step4[n].append(remote(here, here, z_peers[k]))

    def four(ref):
        value = ref[0].astype(F32)
        for i in range(1, 4):
            value = value + ref[i].astype(F32)
        return value.astype(BF16)

    for copy in s2:
        copy.wait_recv()
    sy[y] = four(sx)
    s3 = [remote(sy.at[y], sy.at[y], y_peers[k]) for k in far4]

    step5 = ({}, {})
    step6 = ({}, {})

    def forward(n, m):
        u, v, u_peer = parts[n][6], parts[n][7], parts[n][8]
        block = big.at[place(core, n, u[0], v[(4 - m) % 4], 32)]
        for k in far4:
            step6[n][m, k] = remote(block, block, u_peer[k])

    for n in range(2):
        u, v, v_peer = parts[n][6], parts[n][7], parts[n][9]
        for copy in step4[n]:
            copy.wait_recv()
        block = big.at[place(core, n, u[0], v[0], 32)]
        for k in far4:
            step5[n][k] = remote(block, block, v_peer[k])
    for n in range(2):
        forward(n, 0)

    for copy in s3:
        copy.wait_recv()
    small[core, piece(z, 48), :] = four(sy)
    bit = small.at[core, piece(z, 48)]
    s4 = [remote(bit, bit, z_peers[k]) for k in far]

    for m in (1, 3, 2):
        for n in range(2):
            step5[n][m].wait_recv()
            forward(n, m)

    last = []

    def cross(n, u):
        chunk = place(core, n, u, 0, 128)
        last.append((remote(big.at[chunk], big.at[chunk], sibling), place(other, n, u, 0, 128)))
        keep(big.at[chunk], big_ref.at[chunk])

    for n in range(2):
        cross(n, parts[n][6][0])
    for copy in s4:
        copy.wait_recv()
    bits = remote(small.at[core], small.at[core], sibling)
    keep(small.at[core], small_ref.at[core])
    for k in (1, 3, 2):
        for n in range(2):
            for m in (0, 1, 3, 2):
                step6[n][m, k].wait_recv()
            cross(n, parts[n][6][4 - k])
    bits.wait_recv()
    keep(small.at[other], small_ref.at[other])
    for copy, chunk in last:
        copy.wait_recv()
        keep(big.at[chunk], big_ref.at[chunk])
    for copy in started:
        copy.wait_send()
    for copy in kept:
        copy.wait()


N_SEM = 160
N_KEEP = 24


STEPS = 8


def widen(big_ref, small_ref, loss_ref, in_ref, out_ref, mix_ref, rows_ref, big, wide, small, small32, load_sem, store_sem):
    size = FEATS // STEPS
    loads = []
    stores = [pltpu.make_async_copy(loss_ref, rows_ref, store_sem.at[STEPS])]
    stores[0].start()
    for i in range(STEPS):
        rows = pl.ds(i * size, size)
        loads.append(pltpu.make_async_copy(big_ref.at[rows], big.at[rows], load_sem.at[i]))
    loads.append(pltpu.make_async_copy(small_ref, small, load_sem.at[STEPS]))
    for load in loads:
        load.start()
    for i in range(STEPS):
        rows = pl.ds(i * size, size)
        loads[i].wait()
        wide[rows, :] = big[rows, :].astype(F32)
        stores.append(pltpu.make_async_copy(wide.at[rows], in_ref.at[rows], store_sem.at[i]))
        stores[-1].start()
    loads[STEPS].wait()
    small32[...] = small[...].astype(F32)
    for h in range(2):
        at = small32.at[h, pl.ds(0, 256)]
        stores.append(pltpu.make_async_copy(at, out_ref.at[pl.ds(h * 256, 256)], store_sem.at[STEPS + 1 + h]))
        stores[-1].start()
        at = small32.at[h, pl.ds(256, 128)]
        stores.append(pltpu.make_async_copy(at, mix_ref.at[pl.ds(h * 128, 128)], store_sem.at[STEPS + 3 + h]))
        stores[-1].start()
    for store in stores:
        store.wait()


def on_device(patches, w_mix, w_in, w_out, partner_dev, partner_row):
    vmem = pltpu.VMEM
    any_spec = pl.BlockSpec(memory_space=pl.ANY)
    scratch = [
        vmem((1, COUNT), jnp.int32),
        vmem((1, COUNT), jnp.int32),
        vmem((COUNT * ANGLES, LANES), BF16),
        vmem((256, 512), BF16),
        vmem((LANES, FILTERS), BF16),
        vmem((FEATS, HIDDEN), BF16),
        vmem((HIDDEN, EMBED), BF16),
        vmem((2 * FREQS * COUNT, LANES), BF16),
        vmem((LANES, 2 * FREQS * COUNT), BF16),
        vmem((FREQS * COUNT, FILTERS), F32),
        vmem((FREQS * COUNT, FILTERS), F32),
        vmem((COUNT, FEATS), F32),
        vmem((COUNT, FEATS), BF16),
        vmem((COUNT, HIDDEN), F32),
        vmem((HIDDEN, COUNT), BF16),
        vmem((COUNT, FEATS), F32),
        vmem((2 * FREQS * COUNT, FILTERS), BF16),
        vmem((GROUP, EMBED), BF16),
        vmem((PEERS, SLOT, COUNT), F32),
        vmem((PEERS, SLOT, COUNT), F32),
        vmem((PEERS, SLOT, COUNT), F32),
        vmem((PEERS, SLOT, COUNT), F32),
        vmem((PEERS, SLOT, COUNT), F32),
        vmem((PEERS, SLOT, COUNT), F32),
        vmem((CYCLE * TILE, COUNT), F32),
        vmem((FEATS // 2, COUNT), BF16),
        vmem((FEATS // 2, COUNT), BF16),
        vmem((FEATS // 2, COUNT), BF16),
        vmem((COUNT, HIDDEN), BF16),
        vmem((COUNT, HIDDEN), BF16),
        vmem((512, 512), BF16),
        vmem((512, 512), BF16),
        vmem((3, 128, 512), BF16),
        vmem((3, 128, 512), BF16),
        vmem((128, 512), BF16),
        vmem((128, 512), BF16),
        vmem((3, 32, 512), BF16),
        vmem((3, 32, 512), BF16),
        vmem((32, 512), BF16),
        vmem((32, 512), BF16),
        vmem((7, 16, 128), BF16),
        vmem((7, 16, 128), BF16),
        vmem((2, SMALL, 128), F32),
        vmem((SMALL, 128), F32),
        vmem((SMALL, 128), BF16),
        vmem((7, 48, 128), BF16),
        vmem((4, 48, 128), BF16),
        vmem((4, 48, 128), BF16),
        vmem((FEATS, HIDDEN), BF16),
        vmem((2, SMALL, 128), BF16),
        vmem((1, COUNT), F32),
        pltpu.SemaphoreType.DMA((14,)),
        pltpu.SemaphoreType.DMA((N_KEEP,)),
        pltpu.SemaphoreType.DMA((N_SEM,)),
        pltpu.SemaphoreType.DMA((N_SEM,)),
    ]
    loss, big, small = pl.pallas_call(
        kernel,
        name="contrastive_step",
        out_shape=(
            jax.ShapeDtypeStruct((1, COUNT), F32),
            jax.ShapeDtypeStruct((FEATS, HIDDEN), BF16),
            jax.ShapeDtypeStruct((2, SMALL, 128), BF16),
        ),
        in_specs=[any_spec] * 7,
        out_specs=(any_spec, any_spec, any_spec),
        scratch_shapes=scratch,
        compiler_params=pltpu.CompilerParams(
            collective_id=0, has_side_effects=True, vmem_limit_bytes=56 * 2**20
        ),
    )(
        partner_dev.reshape(1, COUNT),
        partner_row.reshape(1, COUNT),
        jnp.asarray(block_table()),
        w_mix,
        w_in,
        w_out,
        patches.reshape(COUNT * ANGLES, LANES),
    )
    g_in, g_out, g_mix, loss = pl.pallas_call(
        widen,
        name="widen",
        out_shape=(
            jax.ShapeDtypeStruct((FEATS, HIDDEN), F32),
            jax.ShapeDtypeStruct((HIDDEN, EMBED), F32),
            jax.ShapeDtypeStruct((LANES, FILTERS), F32),
            jax.ShapeDtypeStruct((1, COUNT), F32),
        ),
        in_specs=[any_spec] * 3,
        out_specs=(any_spec,) * 4,
        scratch_shapes=[
            vmem((FEATS, HIDDEN), BF16),
            vmem((FEATS, HIDDEN), F32),
            vmem((2, SMALL, 128), BF16),
            vmem((2, SMALL, 128), F32),
            pltpu.SemaphoreType.DMA((STEPS + 1,)),
            pltpu.SemaphoreType.DMA((STEPS + 5,)),
        ],
        compiler_params=pltpu.CompilerParams(vmem_limit_bytes=56 * 2**20),
    )(big, small, loss)
    return (loss.reshape(COUNT), g_mix, g_in, g_out)


def solution(mesh):
    placed = (P(("blk", "dp"), None, None), P(), P(), P(), P(("blk", "dp")), P(("blk", "dp")))
    return jax.shard_map(
        on_device,
        mesh=mesh,
        in_specs=placed,
        out_specs=(P(("blk", "dp")), P(), P(), P()),
        check_vma=False,
    )
```

```python
import functools
import math

import jax
import jax.numpy as jnp
import ml_dtypes
import numpy as np
from jax import lax
from jax.experimental import pallas as pl
from jax.experimental.pallas import tpu as pltpu
from jax.sharding import PartitionSpec as P

SCALE = 10.0
MESH = pl.DeviceIdType.MESH
F32 = jnp.float32
BF16 = jnp.bfloat16

COUNT = 128
ANGLES = 64
LANES = 256
FREQS = 16
FILTERS = 128
FEATS = FREQS * FILTERS
HIDDEN = 512
EMBED = 128
PEERS = 32
CYCLE = 8
GROUP = CYCLE * COUNT
SLOT = COUNT // PEERS
TILE = 8
SMALL = 384
COEF = SCALE / COUNT


def block_table():
    angle = np.arange(ANGLES)
    freq = np.arange(FREQS)
    phase = np.mod(freq[None, :] * angle[:, None], ANGLES).astype(np.float32) * np.float32(
        2.0 * math.pi / ANGLES
    )
    table = np.concatenate([np.cos(phase), -np.sin(phase)], axis=1)
    wide = np.zeros((2 * FREQS, 4, 4, ANGLES), np.float32)
    for n in range(4):
        wide[:, n, n, :] = table.T
    return wide.reshape(2 * FREQS * 4, 4 * ANGLES).astype(ml_dtypes.bfloat16)


def dot(a, b):
    return jnp.dot(a, b, preferred_element_type=F32)


def dot_t(a, b):
    return lax.dot_general(a, b, (((1,), (1,)), ((), ())), preferred_element_type=F32)


def split(v):
    high = v.astype(BF16)
    return high, (v - high.astype(F32)).astype(BF16)


def iota(shape, dim):
    return lax.broadcasted_iota(jnp.int32, shape, dim)


def kernel(
    pdev_hbm, prow_hbm, table_hbm, wmix_hbm, win_hbm, wout_hbm, patches_hbm,
    loss_ref, big_ref, small_ref,
    pdev_ref, prow_ref, patches, table, wmix, win, wout,
    spec, spec_t, real, imag, feat, normed, preact, hid_t, ngrad, mixg,
    group, ask_out, ask_in, row_out, row_in, back_out, back_in, tot_all,
    nt_own, nt_send, nt_sib, gp_own, gp_sib,
    pa, pb, ra1, rb1, pa2, pb2, ra2, rb2, cells, cells_in, done,
    sm, sm_sib, sm0, sz, sx, sy,
    big, small, loss,
    load_sem, keep_sem, send_sem, recv_sem,
):
    blk = lax.axis_index("blk")
    dp = lax.axis_index("dp")
    y = lax.div(blk, 2)
    x_low = lax.div(dp, 16)
    x = lax.rem(blk, 2) * 2 + x_low
    z = lax.rem(lax.div(dp, 2), 8)
    core = lax.rem(dp, 2)
    other = 1 - core

    def device(x_, y_, z_, c_):
        return (y_ * 2 + lax.div(x_, 2), lax.rem(x_, 2) * 16 + z_ * 2 + c_)

    sibling = device(x, y, z, other)

    dp_peers = []
    for dz in (4, 5, 3, 6, 2, 7, 1, 0):
        z_part = lax.rem(z + dz, 8) * 2
        for x_part in ((1 - x_low) * 16, x_low * 16):
            for c_part in (other, core):
                dp_peers.append(x_part + z_part + c_part)
    dp_peers = dp_peers[:-1]
    blk_peers = [lax.rem(blk + step, CYCLE) for step in (5, 4, 3, 2, 1, 6, 7)]

    used = [0]
    started = []

    def remote(src, dst, to):
        k = used[0]
        used[0] += 1
        copy = pltpu.make_async_remote_copy(
            src_ref=src, dst_ref=dst, send_sem=send_sem.at[k], recv_sem=recv_sem.at[k],
            device_id=to, device_id_type=MESH,
        )
        copy.start()
        started.append(copy)
        return copy

    def spread(value, src, dst):
        k = used[0]
        used[0] += 1
        for p in range(PEERS):
            src[p] = value[p * SLOT : (p + 1) * SLOT]

        for p in dp_peers:
            pltpu.make_async_remote_copy(
                src_ref=src.at[p], dst_ref=dst.at[dp],
                send_sem=send_sem.at[k], recv_sem=recv_sem.at[k],
                device_id=(blk, p), device_id_type=MESH,
            ).start()
        dst[dp] = src[dp]
        rows = pl.ds(0, PEERS - 1)
        whole = pltpu.make_async_remote_copy(
            src_ref=src.at[rows], dst_ref=dst.at[rows], send_sem=send_sem.at[k],
            recv_sem=recv_sem.at[k], device_id=(blk, dp_peers[0]), device_id_type=MESH,
        )
        started.append(whole)
        return whole

    def flat(ref):
        return jnp.concatenate([ref[p] for p in range(PEERS)], axis=0)

    def to_group(ref, rows):
        k = used[0]
        used[0] += 1
        mine = pl.ds(pl.multiple_of(blk * rows, rows), rows)
        for b in blk_peers:
            pltpu.make_async_remote_copy(
                src_ref=ref.at[mine], dst_ref=ref.at[mine],
                send_sem=send_sem.at[k], recv_sem=recv_sem.at[k],
                device_id=(b, dp), device_id_type=MESH,
            ).start()
        span = pl.ds(0, (CYCLE - 1) * rows)
        whole = pltpu.make_async_remote_copy(
            src_ref=ref.at[span], dst_ref=ref.at[span], send_sem=send_sem.at[k],
            recv_sem=recv_sem.at[k], device_id=(blk_peers[0], dp), device_id_type=MESH,
        )
        started.append(whole)
        return whole

    kept = []

    def keep(src, dst):
        copy = pltpu.make_async_copy(src, dst, keep_sem.at[len(kept)])
        copy.start()
        kept.append(copy)

    barrier = pltpu.get_barrier_semaphore()

    for p in dp_peers:
        pl.semaphore_signal(barrier, inc=1, device_id=(blk, p), device_id_type=MESH)
    for b in blk_peers:
        pl.semaphore_signal(barrier, inc=1, device_id=(b, dp), device_id_type=MESH)
    pl.semaphore_signal(barrier, inc=1, device_id=device(3 - x, y, z, core), device_id_type=MESH)

    chunk = 1024
    loads = [pltpu.make_async_copy(table_hbm, table, load_sem.at[0])]
    for g in range(8):
        rows = pl.ds(g * chunk, chunk)
        loads.append(pltpu.make_async_copy(patches_hbm.at[rows], patches.at[rows], load_sem.at[1 + g]))
    loads.append(pltpu.make_async_copy(wmix_hbm, wmix, load_sem.at[9]))
    loads.append(pltpu.make_async_copy(win_hbm, win, load_sem.at[10]))
    loads.append(pltpu.make_async_copy(wout_hbm, wout, load_sem.at[11]))
    loads.append(pltpu.make_async_copy(pdev_hbm, pdev_ref, load_sem.at[12]))
    loads.append(pltpu.make_async_copy(prow_hbm, prow_ref, load_sem.at[13]))
    for i in (12, 13) + tuple(range(12)):
        loads[i].start()

    loads[12].wait()
    loads[13].wait()
    lane = iota((COUNT, COUNT), 1)
    row = iota((COUNT, COUNT), 0)
    dev_lane = jnp.broadcast_to(pdev_ref[...], (COUNT, COUNT))
    dev_row = dev_lane.astype(F32).T.astype(jnp.int32)
    same = dev_lane == dev_row
    rank_lane = jnp.sum(jnp.where(same & (row < lane), 1.0, 0.0), axis=0, keepdims=True)
    rank_row = jnp.sum(jnp.where(same & (lane < row), 1.0, 0.0), axis=1, keepdims=True)
    place_lane = pdev_ref[...] * SLOT + rank_lane.astype(jnp.int32)
    place_row = dev_row[:, :1] * SLOT + rank_row.astype(jnp.int32)
    to_slot = jnp.where(
        iota((PEERS * SLOT, COUNT), 0) == place_lane, 1.0, 0.0
    ).astype(BF16)
    from_slot = jnp.where(
        iota((COUNT, PEERS * SLOT), 1) == place_row, 1.0, 0.0
    ).astype(BF16)
    prow = jnp.broadcast_to(prow_ref[...], (COUNT, COUNT)).astype(F32).T.astype(BF16)
    ask = dot(to_slot, prow)

    loads[0].wait()
    bank = table[...]
    for g in range(8):
        loads[1 + g].wait()
        quads = [dot(bank, patches[g * chunk + q * 256 : g * chunk + (q + 1) * 256, :]) for q in range(4)]
        for k in range(2 * FREQS):
            part = jnp.concatenate([quad[k * 4 : k * 4 + 4] for quad in quads], axis=0)
            spec[k * COUNT + g * 16 : k * COUNT + g * 16 + 16, :] = part.astype(BF16)
        if g == 2:
            pl.semaphore_wait(barrier, PEERS - 1 + CYCLE - 1 + 1)
            asked = spread(ask, ask_out, ask_in)

    loads[9].wait()
    total = jnp.zeros((COUNT, 1), F32)
    for k in range(0, FREQS, 4):
        rows = slice(k * COUNT, (k + 4) * COUNT)
        re = dot(spec[rows, :], wmix[...])
        im = dot(spec[(FREQS + k) * COUNT : (FREQS + k + 4) * COUNT, :], wmix[...])
        real[rows, :] = re
        imag[rows, :] = im
        value = jnp.log1p(re * re + im * im)
        acc = jnp.zeros((COUNT, FILTERS), F32)
        for i in range(4):
            piece = value[i * COUNT : (i + 1) * COUNT]
            feat[:, (k + i) * FILTERS : (k + i + 1) * FILTERS] = piece
            acc = acc + piece
        total = total + jnp.sum(acc, axis=1, keepdims=True)
    mean = total * (1.0 / FEATS)
    acc = jnp.zeros((COUNT, FILTERS), F32)
    for k in range(FREQS):
        off = feat[:, k * FILTERS : (k + 1) * FILTERS] - mean
        acc = acc + off * off
    rscale = lax.rsqrt(jnp.sum(acc, axis=1, keepdims=True) * (1.0 / FEATS) + 1e-05)
    for k in range(FREQS):
        cols = slice(k * FILTERS, (k + 1) * FILTERS)
        hat = (feat[:, cols] - mean) * rscale
        feat[:, cols] = hat
        normed[:, cols] = hat.astype(BF16)

    loads[10].wait()
    pre = dot(normed[...], win[...])
    preact[...] = pre
    hidden = (pre * jax.nn.sigmoid(pre)).astype(BF16)
    loads[11].wait()
    raw = dot(hidden, wout[...])
    norms = jnp.sqrt(jnp.sum(raw * raw, axis=1, keepdims=True) + 1e-06)
    unit32 = raw / norms
    units = unit32.astype(BF16)
    group[pl.ds(pl.multiple_of(blk * COUNT, COUNT), COUNT), :] = units
    gathered = to_group(group, COUNT)

    asked.wait_recv()
    pick32 = jnp.where(flat(ask_in) == lane.astype(F32), 1.0, 0.0)
    returned = spread(dot(pick32.astype(BF16), units), row_out, row_in)

    unpick = pick32.T.astype(BF16)
    base = core * (FEATS // 2)
    for k in range(8):
        cols = pl.ds(pl.multiple_of((1 - core) * (FEATS // 2) + k * FILTERS, FILTERS), FILTERS)
        nt_send[k * FILTERS : (k + 1) * FILTERS, :] = normed[:, cols].T
    factor = remote(nt_send, nt_sib, sibling)
    for k in range(8):
        cols = pl.ds(pl.multiple_of(base + k * FILTERS, FILTERS), FILTERS)
        nt_own[k * FILTERS : (k + 1) * FILTERS, :] = normed[:, cols].T

    gathered.wait_recv()
    keys = group[...]
    scores = SCALE * dot_t(units, keys)
    self_lane = blk * COUNT + iota((COUNT, GROUP), 0)
    expo = jnp.where(iota((COUNT, GROUP), 1) == self_lane, 0.0, jnp.exp(scores))
    zneg = jnp.sum(expo, axis=1, keepdims=True)
    numer = dot(expo.astype(BF16), keys)

    returned.wait_recv()
    positive = dot(from_slot, flat(row_in).astype(BF16))
    own = units.astype(F32)
    spos = SCALE * jnp.sum(own * positive, axis=1, keepdims=True)
    epos = jnp.exp(spos)
    totals = epos + zneg
    tot_lane = jnp.broadcast_to(totals, (COUNT, COUNT)).T
    tot_all[pl.ds(pl.multiple_of(blk * TILE, TILE), TILE), :] = tot_lane[:TILE]
    tots = to_group(tot_all, TILE)
    away = COEF * (epos / totals - 1.0)
    high, low = split(away * own)
    backs = spread(dot(to_slot, high) + dot(to_slot, low), back_out, back_in)
    spos_lane = jnp.broadcast_to(spos, (COUNT, COUNT)).T
    loss[...] = (jnp.log(tot_lane) - spos_lane)[:1]
    keep(loss, loss_ref)
    grad_units = away * positive + COEF * (numer / totals)
    hid_t[...] = hidden.T
    for k in range(2 * FREQS):
        spec_t[:, k * COUNT : (k + 1) * COUNT] = spec[k * COUNT : (k + 1) * COUNT, :].T

    tots.wait_recv()
    inverse = jnp.concatenate(
        [1.0 / tot_all[b * TILE : b * TILE + 1, :] for b in range(CYCLE)], axis=1
    )
    keyterm = dot((expo * inverse).astype(BF16), keys)
    grad_units = grad_units + COEF * keyterm
    backs.wait_recv()
    high, low = split(flat(back_in))
    grad_units = grad_units + (dot(unpick, high) + dot(unpick, low))

    grad_raw = (
        (grad_units - unit32 * jnp.sum(unit32 * grad_units, axis=1, keepdims=True)) / norms
    ).astype(BF16)
    grad_hid = dot_t(grad_raw, wout[...])
    pre = preact[...]
    sigm = jax.nn.sigmoid(pre)
    grad_pre = (grad_hid * sigm * (1.0 + pre * (1.0 - sigm))).astype(BF16)
    gp_own[...] = grad_pre
    sent = remote(gp_own, gp_sib, sibling)
    g_out = dot(hid_t[...], grad_raw)
    sm[0, 0:256, :] = g_out[:256]
    sm[1, 0:256, :] = g_out[256:]
    ngrad[...] = dot_t(grad_pre, win[...])

    factor.wait_recv()
    sent.wait_recv()
    right = jnp.concatenate([gp_own[...], gp_sib[...]], axis=0)
    def multiply(to, n):
        for i in range(2):
            rows = slice(n * 512 + i * 256, n * 512 + (i + 1) * 256)
            prod = dot(jnp.concatenate([nt_own[rows, :], nt_sib[rows, :]], axis=1), right)
            to[i * 256 : (i + 1) * 256, :] = prod.astype(BF16)

    xs = [lax.rem(x + k, 4) for k in range(4)]
    ys = [lax.rem(y + k, 4) for k in range(4)]
    zs = [lax.rem(z + k, 8) for k in range(8)]
    x_peers = [device(xs[k], y, z, core) for k in range(4)]
    y_peers = [device(x, ys[k], z, core) for k in range(4)]
    z_peers = [device(x, y, zs[k], core) for k in range(8)]

    def piece(at, rows):
        return pl.ds(pl.multiple_of(at * rows, rows), rows)

    parts = (
        (pa, ra1, pa2, ra2, xs, ys, x_peers, y_peers),
        (pb, rb1, pb2, rb2, ys, xs, y_peers, x_peers),
    )
    far4 = (2, 1, 3)
    far = (4, 3, 5, 2, 6, 1, 7)
    step1 = ({}, {})
    for n, (src, got, _, _, u, v, u_peer, _) in enumerate(parts):
        multiply(src, n)
        for j in (2, 1, 3, 0):
            for k in far4:
                step1[n][j, k] = remote(
                    src.at[piece(u[k] * 4 + v[j], 32)],
                    got.at[k - 1, piece(v[j], 32)],
                    u_peer[k],
                )

    acc = jnp.zeros((COUNT, FILTERS), F32)
    acc_hat = jnp.zeros((COUNT, FILTERS), F32)
    for k in range(FREQS):
        cols = slice(k * FILTERS, (k + 1) * FILTERS)
        ng = ngrad[:, cols]
        acc = acc + ng
        acc_hat = acc_hat + ng * feat[:, cols]
    mean_ng = jnp.sum(acc, axis=1, keepdims=True) * (1.0 / FEATS)
    mean_hat = jnp.sum(acc_hat, axis=1, keepdims=True) * (1.0 / FEATS)
    for k in range(FREQS):
        cols = slice(k * FILTERS, (k + 1) * FILTERS)
        rows = slice(k * COUNT, (k + 1) * COUNT)
        re = real[rows, :]
        im = imag[rows, :]
        grad_feat = rscale * (ngrad[:, cols] - mean_ng - feat[:, cols] * mean_hat)
        grad_pow = 2.0 * grad_feat / (1.0 + (re * re + im * im))
        mixg[rows, :] = (re * grad_pow).astype(BF16)
        mixg[(FREQS + k) * COUNT : (FREQS + k + 1) * COUNT, :] = (im * grad_pow).astype(BF16)
    g_mix = dot(spec_t[...], mixg[...])
    sm[0, 256:384, :] = g_mix[:128]
    sm[1, 256:384, :] = g_mix[128:]
    halves = remote(sm.at[other], sm_sib, sibling)

    def add(own_part, got, copies):
        value = own_part.astype(F32)
        for k in sorted(copies):
            copies[k].wait_recv()
            value = value + got[k - 1].astype(F32)
        return value.astype(BF16)

    step2 = ({}, {})
    for j in (2, 1, 3, 0):
        for n, (src, got, src2, got2, u, v, _, v_peer) in enumerate(parts):
            mine = piece(v[j], 32)
            value = src[piece(u[0] * 4 + v[j], 32), :].astype(F32)
            for k in (1, 3, 2):
                step1[n][j, k].wait_recv()
                value = value + got[k - 1, mine, :].astype(F32)
            src2[mine, :] = value.astype(BF16)
            if j:
                step2[n][j] = remote(src2.at[mine], got2.at[j - 1], v_peer[j])

    halves.wait_recv()
    sm0[...] = (sm[core] + sm_sib[...]).astype(BF16)
    s1 = {k: remote(sm0.at[piece(zs[k], 48)], sz.at[k - 1], z_peers[k]) for k in far}

    for n, (_, _, src2, got2, _, v, _, _) in enumerate(parts):
        value = add(src2[piece(v[0], 32), :], got2, step2[n])
        for at in range(8):
            cells[at, n * 16 : n * 16 + 16, :] = value[
                at // 4 * 16 : at // 4 * 16 + 16, at % 4 * 128 : at % 4 * 128 + 128
            ]
    step3 = {k: remote(cells.at[zs[k]], cells_in.at[k - 1], z_peers[k]) for k in far}

    sx[x] = add(sm0[piece(z, 48), :], sz, s1)
    s2 = [remote(sx.at[x], sx.at[x], x_peers[k]) for k in far4]

    def place(c, n, u, v, rows):
        return pl.ds(pl.multiple_of(c * 1024 + n * 512 + u * 128 + v * 32, 32), rows)

    done[z] = add(cells[z], cells_in, step3)
    step4 = [remote(done.at[z], done.at[z], z_peers[k]) for k in far]

    def four(ref):
        value = ref[0].astype(F32)
        for i in range(1, 4):
            value = value + ref[i].astype(F32)
        return value.astype(BF16)

    for copy in s2:
        copy.wait_recv()
    sy[y] = four(sx)
    s3 = [remote(sy.at[y], sy.at[y], y_peers[k]) for k in far4]

    step5 = ({}, {})
    step6 = ({}, {})

    def forward(n, m):
        u, v, u_peer = parts[n][4], parts[n][5], parts[n][6]
        block = big.at[place(core, n, u[0], v[(4 - m) % 4], 32)]
        for k in far4:
            step6[n][m, k] = remote(block, block, u_peer[k])

    for copy in step4:
        copy.wait_recv()
    for n in range(2):
        u, v, v_peer = parts[n][4], parts[n][5], parts[n][7]
        for at in range(8):
            rows = pl.ds(pl.multiple_of(core * 1024 + n * 512 + u[0] * 128 + v[0] * 32 + at // 4 * 16, 16), 16)
            big[rows, at % 4 * 128 : at % 4 * 128 + 128] = done[at, n * 16 : n * 16 + 16, :]
        block = big.at[place(core, n, u[0], v[0], 32)]
        for k in far4:
            step5[n][k] = remote(block, block, v_peer[k])
    for n in range(2):
        forward(n, 0)

    for copy in s3:
        copy.wait_recv()
    small[core, piece(z, 48), :] = four(sy)
    bit = small.at[core, piece(z, 48)]
    s4 = [remote(bit, bit, z_peers[k]) for k in far]

    for m in (1, 3, 2):
        for n in range(2):
            step5[n][m].wait_recv()
            forward(n, m)

    last = []

    def cross(n, u):
        chunk = place(core, n, u, 0, 128)
        last.append(remote(big.at[chunk], big_ref.at[chunk], sibling))
        keep(big.at[chunk], big_ref.at[chunk])

    for n in range(2):
        cross(n, parts[n][4][0])
    for copy in s4:
        copy.wait_recv()
    last.append(remote(small.at[core], small_ref.at[core], sibling))
    keep(small.at[core], small_ref.at[core])
    for k in (1, 3, 2):
        for n in range(2):
            for m in (0, 1, 3, 2):
                step6[n][m, k].wait_recv()
            cross(n, parts[n][4][4 - k])
    for copy in last:
        copy.wait_recv()
    for copy in started:
        copy.wait_send()
    for copy in kept:
        copy.wait()


N_SEM = 160
N_KEEP = 24


STEPS = 8


def widen(big_ref, small_ref, loss_ref, in_ref, out_ref, mix_ref, rows_ref, big, wide, small, small32, load_sem, store_sem):
    size = FEATS // STEPS
    loads = []
    stores = [pltpu.make_async_copy(loss_ref, rows_ref, store_sem.at[STEPS])]
    stores[0].start()
    for i in range(STEPS):
        rows = pl.ds(i * size, size)
        loads.append(pltpu.make_async_copy(big_ref.at[rows], big.at[rows], load_sem.at[i]))
    loads.append(pltpu.make_async_copy(small_ref, small, load_sem.at[STEPS]))
    for load in loads:
        load.start()
    for i in range(STEPS):
        rows = pl.ds(i * size, size)
        loads[i].wait()
        wide[rows, :] = big[rows, :].astype(F32)
        stores.append(pltpu.make_async_copy(wide.at[rows], in_ref.at[rows], store_sem.at[i]))
        stores[-1].start()
    loads[STEPS].wait()
    small32[...] = small[...].astype(F32)
    for h in range(2):
        at = small32.at[h, pl.ds(0, 256)]
        stores.append(pltpu.make_async_copy(at, out_ref.at[pl.ds(h * 256, 256)], store_sem.at[STEPS + 1 + h]))
        stores[-1].start()
        at = small32.at[h, pl.ds(256, 128)]
        stores.append(pltpu.make_async_copy(at, mix_ref.at[pl.ds(h * 128, 128)], store_sem.at[STEPS + 3 + h]))
        stores[-1].start()
    for store in stores:
        store.wait()


def on_device(patches, w_mix, w_in, w_out, partner_dev, partner_row):
    vmem = pltpu.VMEM
    any_spec = pl.BlockSpec(memory_space=pl.ANY)
    scratch = [
        vmem((1, COUNT), jnp.int32),
        vmem((1, COUNT), jnp.int32),
        vmem((COUNT * ANGLES, LANES), BF16),
        vmem((128, 256), BF16),
        vmem((LANES, FILTERS), BF16),
        vmem((FEATS, HIDDEN), BF16),
        vmem((HIDDEN, EMBED), BF16),
        vmem((2 * FREQS * COUNT, LANES), BF16),
        vmem((LANES, 2 * FREQS * COUNT), BF16),
        vmem((FREQS * COUNT, FILTERS), F32),
        vmem((FREQS * COUNT, FILTERS), F32),
        vmem((COUNT, FEATS), F32),
        vmem((COUNT, FEATS), BF16),
        vmem((COUNT, HIDDEN), F32),
        vmem((HIDDEN, COUNT), BF16),
        vmem((COUNT, FEATS), F32),
        vmem((2 * FREQS * COUNT, FILTERS), BF16),
        vmem((GROUP, EMBED), BF16),
        vmem((PEERS, SLOT, COUNT), F32),
        vmem((PEERS, SLOT, COUNT), F32),
        vmem((PEERS, SLOT, COUNT), F32),
        vmem((PEERS, SLOT, COUNT), F32),
        vmem((PEERS, SLOT, COUNT), F32),
        vmem((PEERS, SLOT, COUNT), F32),
        vmem((CYCLE * TILE, COUNT), F32),
        vmem((FEATS // 2, COUNT), BF16),
        vmem((FEATS // 2, COUNT), BF16),
        vmem((FEATS // 2, COUNT), BF16),
        vmem((COUNT, HIDDEN), BF16),
        vmem((COUNT, HIDDEN), BF16),
        vmem((512, 512), BF16),
        vmem((512, 512), BF16),
        vmem((3, 128, 512), BF16),
        vmem((3, 128, 512), BF16),
        vmem((128, 512), BF16),
        vmem((128, 512), BF16),
        vmem((3, 32, 512), BF16),
        vmem((3, 32, 512), BF16),
        vmem((8, 32, 128), BF16),
        vmem((7, 32, 128), BF16),
        vmem((8, 32, 128), BF16),
        vmem((2, SMALL, 128), F32),
        vmem((SMALL, 128), F32),
        vmem((SMALL, 128), BF16),
        vmem((7, 48, 128), BF16),
        vmem((4, 48, 128), BF16),
        vmem((4, 48, 128), BF16),
        vmem((FEATS, HIDDEN), BF16),
        vmem((2, SMALL, 128), BF16),
        vmem((1, COUNT), F32),
        pltpu.SemaphoreType.DMA((14,)),
        pltpu.SemaphoreType.DMA((N_KEEP,)),
        pltpu.SemaphoreType.DMA((N_SEM,)),
        pltpu.SemaphoreType.DMA((N_SEM,)),
    ]
    loss, big, small = pl.pallas_call(
        kernel,
        name="contrastive_step",
        out_shape=(
            jax.ShapeDtypeStruct((1, COUNT), F32),
            jax.ShapeDtypeStruct((FEATS, HIDDEN), BF16),
            jax.ShapeDtypeStruct((2, SMALL, 128), BF16),
        ),
        in_specs=[any_spec] * 7,
        out_specs=(any_spec, any_spec, any_spec),
        scratch_shapes=scratch,
        compiler_params=pltpu.CompilerParams(
            collective_id=0, has_side_effects=True, vmem_limit_bytes=56 * 2**20
        ),
    )(
        partner_dev.reshape(1, COUNT),
        partner_row.reshape(1, COUNT),
        jnp.asarray(block_table()),
        w_mix,
        w_in,
        w_out,
        patches.reshape(COUNT * ANGLES, LANES),
    )
    g_in, g_out, g_mix, loss = pl.pallas_call(
        widen,
        name="widen",
        out_shape=(
            jax.ShapeDtypeStruct((FEATS, HIDDEN), F32),
            jax.ShapeDtypeStruct((HIDDEN, EMBED), F32),
            jax.ShapeDtypeStruct((LANES, FILTERS), F32),
            jax.ShapeDtypeStruct((1, COUNT), F32),
        ),
        in_specs=[any_spec] * 3,
        out_specs=(any_spec,) * 4,
        scratch_shapes=[
            vmem((FEATS, HIDDEN), BF16),
            vmem((FEATS, HIDDEN), F32),
            vmem((2, SMALL, 128), BF16),
            vmem((2, SMALL, 128), F32),
            pltpu.SemaphoreType.DMA((STEPS + 1,)),
            pltpu.SemaphoreType.DMA((STEPS + 5,)),
        ],
        compiler_params=pltpu.CompilerParams(vmem_limit_bytes=56 * 2**20),
    )(big, small, loss)
    return (loss.reshape(COUNT), g_mix, g_in, g_out)


def solution(mesh):
    placed = (P(("blk", "dp"), None, None), P(), P(), P(), P(("blk", "dp")), P(("blk", "dp")))
    return jax.shard_map(
        on_device,
        mesh=mesh,
        in_specs=placed,
        out_specs=(P(("blk", "dp")), P(), P(), P()),
        check_vma=False,
    )
```

```python
import functools
import math

import jax
import jax.numpy as jnp
import ml_dtypes
import numpy as np
from jax import lax
from jax.experimental import pallas as pl
from jax.experimental.pallas import tpu as pltpu
from jax.sharding import PartitionSpec as P

SCALE = 10.0
MESH = pl.DeviceIdType.MESH
F32 = jnp.float32
BF16 = jnp.bfloat16

COUNT = 128
ANGLES = 64
LANES = 256
FREQS = 16
FILTERS = 128
FEATS = FREQS * FILTERS
HIDDEN = 512
EMBED = 128
PEERS = 32
CYCLE = 8
GROUP = CYCLE * COUNT
SLOT = COUNT // PEERS
TILE = 8
SMALL = 384
COEF = SCALE / COUNT


def block_table():
    angle = np.arange(ANGLES)
    freq = np.arange(FREQS)
    phase = np.mod(freq[None, :] * angle[:, None], ANGLES).astype(np.float32) * np.float32(
        2.0 * math.pi / ANGLES
    )
    table = np.concatenate([np.cos(phase), -np.sin(phase)], axis=1)
    wide = np.zeros((2 * FREQS, 4, 4, ANGLES), np.float32)
    for n in range(4):
        wide[:, n, n, :] = table.T
    return wide.reshape(2 * FREQS * 4, 4 * ANGLES).astype(ml_dtypes.bfloat16)


def dot(a, b):
    return jnp.dot(a, b, preferred_element_type=F32)


def dot_t(a, b):
    return lax.dot_general(a, b, (((1,), (1,)), ((), ())), preferred_element_type=F32)


def split(v):
    high = v.astype(BF16)
    return high, (v - high.astype(F32)).astype(BF16)


def iota(shape, dim):
    return lax.broadcasted_iota(jnp.int32, shape, dim)


def kernel(
    pdev_hbm, prow_hbm, table_hbm, wmix_hbm, win_hbm, wout_hbm, patches_hbm,
    loss_ref, big_ref, small_ref,
    pdev_ref, prow_ref, patches, table, wmix, win, wout,
    spec, spec_t, real, imag, feat, normed, preact, hid_t, ngrad, mixg,
    group, ask_out, ask_in, row_out, row_in, back_out, back_in, tot_all,
    nt_own, nt_send, nt_sib, gp_own, gp_sib,
    pa, pb, ra1, rb1, pa2, pb2, ra2, rb2, cells, cells_in, done,
    sm, sm_sib, sm0, sz, sx, sy,
    big, small, loss,
    load_sem, keep_sem, send_sem, recv_sem,
):
    blk = lax.axis_index("blk")
    dp = lax.axis_index("dp")
    y = lax.div(blk, 2)
    x_low = lax.div(dp, 16)
    x = lax.rem(blk, 2) * 2 + x_low
    z = lax.rem(lax.div(dp, 2), 8)
    core = lax.rem(dp, 2)
    other = 1 - core

    def device(x_, y_, z_, c_):
        return (y_ * 2 + lax.div(x_, 2), lax.rem(x_, 2) * 16 + z_ * 2 + c_)

    sibling = device(x, y, z, other)

    dp_peers = []
    for dz in (4, 5, 3, 6, 2, 7, 1, 0):
        z_part = lax.rem(z + dz, 8) * 2
        for x_part in ((1 - x_low) * 16, x_low * 16):
            for c_part in (other, core):
                dp_peers.append(x_part + z_part + c_part)
    dp_peers = dp_peers[:-1]
    blk_peers = [lax.rem(blk + step, CYCLE) for step in (5, 4, 3, 2, 1, 6, 7)]

    used = [0]
    started = []

    settled = [0]

    def settle(upto):
        for copy in started[settled[0] : upto]:
            copy.wait_send()
        settled[0] = max(settled[0], upto)

    def remote(src, dst, to):
        k = used[0]
        used[0] += 1
        copy = pltpu.make_async_remote_copy(
            src_ref=src, dst_ref=dst, send_sem=send_sem.at[k], recv_sem=recv_sem.at[k],
            device_id=to, device_id_type=MESH,
        )
        copy.start()
        started.append(copy)
        return copy

    def spread(value, src, dst):
        k = used[0]
        used[0] += 1
        for p in range(PEERS):
            src[p] = value[p * SLOT : (p + 1) * SLOT]

        for p in dp_peers:
            pltpu.make_async_remote_copy(
                src_ref=src.at[p], dst_ref=dst.at[dp],
                send_sem=send_sem.at[k], recv_sem=recv_sem.at[k],
                device_id=(blk, p), device_id_type=MESH,
            ).start()
        dst[dp] = src[dp]
        rows = pl.ds(0, PEERS - 1)
        whole = pltpu.make_async_remote_copy(
            src_ref=src.at[rows], dst_ref=dst.at[rows], send_sem=send_sem.at[k],
            recv_sem=recv_sem.at[k], device_id=(blk, dp_peers[0]), device_id_type=MESH,
        )
        started.append(whole)
        return whole

    def flat(ref):
        return jnp.concatenate([ref[p] for p in range(PEERS)], axis=0)

    def to_group(ref, rows):
        k = used[0]
        used[0] += 1
        mine = pl.ds(pl.multiple_of(blk * rows, rows), rows)
        for b in blk_peers:
            pltpu.make_async_remote_copy(
                src_ref=ref.at[mine], dst_ref=ref.at[mine],
                send_sem=send_sem.at[k], recv_sem=recv_sem.at[k],
                device_id=(b, dp), device_id_type=MESH,
            ).start()
        span = pl.ds(0, (CYCLE - 1) * rows)
        whole = pltpu.make_async_remote_copy(
            src_ref=ref.at[span], dst_ref=ref.at[span], send_sem=send_sem.at[k],
            recv_sem=recv_sem.at[k], device_id=(blk_peers[0], dp), device_id_type=MESH,
        )
        started.append(whole)
        return whole

    kept = []

    def keep(src, dst):
        copy = pltpu.make_async_copy(src, dst, keep_sem.at[len(kept)])
        copy.start()
        kept.append(copy)

    barrier = pltpu.get_barrier_semaphore()

    for p in dp_peers:
        pl.semaphore_signal(barrier, inc=1, device_id=(blk, p), device_id_type=MESH)
    for b in blk_peers:
        pl.semaphore_signal(barrier, inc=1, device_id=(b, dp), device_id_type=MESH)
    pl.semaphore_signal(barrier, inc=1, device_id=device(3 - x, y, z, core), device_id_type=MESH)

    chunk = 1024
    loads = [pltpu.make_async_copy(table_hbm, table, load_sem.at[0])]
    for g in range(8):
        rows = pl.ds(g * chunk, chunk)
        loads.append(pltpu.make_async_copy(patches_hbm.at[rows], patches.at[rows], load_sem.at[1 + g]))
    loads.append(pltpu.make_async_copy(wmix_hbm, wmix, load_sem.at[9]))
    loads.append(pltpu.make_async_copy(win_hbm, win, load_sem.at[10]))
    loads.append(pltpu.make_async_copy(wout_hbm, wout, load_sem.at[11]))
    loads.append(pltpu.make_async_copy(pdev_hbm, pdev_ref, load_sem.at[12]))
    loads.append(pltpu.make_async_copy(prow_hbm, prow_ref, load_sem.at[13]))
    for i in (12, 13) + tuple(range(12)):
        loads[i].start()

    loads[12].wait()
    loads[13].wait()
    lane = iota((COUNT, COUNT), 1)
    row = iota((COUNT, COUNT), 0)
    dev_lane = jnp.broadcast_to(pdev_ref[...], (COUNT, COUNT))
    dev_row = dev_lane.astype(F32).T.astype(jnp.int32)
    same = dev_lane == dev_row
    rank_lane = jnp.sum(jnp.where(same & (row < lane), 1.0, 0.0), axis=0, keepdims=True)
    rank_row = jnp.sum(jnp.where(same & (lane < row), 1.0, 0.0), axis=1, keepdims=True)
    place_lane = pdev_ref[...] * SLOT + rank_lane.astype(jnp.int32)
    place_row = dev_row[:, :1] * SLOT + rank_row.astype(jnp.int32)
    to_slot = jnp.where(
        iota((PEERS * SLOT, COUNT), 0) == place_lane, 1.0, 0.0
    ).astype(BF16)
    from_slot = jnp.where(
        iota((COUNT, PEERS * SLOT), 1) == place_row, 1.0, 0.0
    ).astype(BF16)
    prow = jnp.broadcast_to(prow_ref[...], (COUNT, COUNT)).astype(F32).T.astype(BF16)
    ask = dot(to_slot, prow)

    loads[0].wait()
    bank = table[...]
    for g in range(8):
        loads[1 + g].wait()
        quads = [dot(bank, patches[g * chunk + q * 256 : g * chunk + (q + 1) * 256, :]) for q in range(4)]
        for k in range(2 * FREQS):
            part = jnp.concatenate([quad[k * 4 : k * 4 + 4] for quad in quads], axis=0)
            spec[k * COUNT + g * 16 : k * COUNT + g * 16 + 16, :] = part.astype(BF16)
        if g == 2:
            pl.semaphore_wait(barrier, PEERS - 1 + CYCLE - 1 + 1)
            asked = spread(ask, ask_out, ask_in)

    loads[9].wait()
    total = jnp.zeros((COUNT, 1), F32)
    for k in range(0, FREQS, 4):
        rows = slice(k * COUNT, (k + 4) * COUNT)
        re = dot(spec[rows, :], wmix[...])
        im = dot(spec[(FREQS + k) * COUNT : (FREQS + k + 4) * COUNT, :], wmix[...])
        real[rows, :] = re
        imag[rows, :] = im
        value = jnp.log1p(re * re + im * im)
        acc = jnp.zeros((COUNT, FILTERS), F32)
        for i in range(4):
            piece = value[i * COUNT : (i + 1) * COUNT]
            feat[:, (k + i) * FILTERS : (k + i + 1) * FILTERS] = piece
            acc = acc + piece
        total = total + jnp.sum(acc, axis=1, keepdims=True)
    mean = total * (1.0 / FEATS)
    acc = jnp.zeros((COUNT, FILTERS), F32)
    for k in range(FREQS):
        off = feat[:, k * FILTERS : (k + 1) * FILTERS] - mean
        acc = acc + off * off
    rscale = lax.rsqrt(jnp.sum(acc, axis=1, keepdims=True) * (1.0 / FEATS) + 1e-05)
    for k in range(FREQS):
        cols = slice(k * FILTERS, (k + 1) * FILTERS)
        hat = (feat[:, cols] - mean) * rscale
        feat[:, cols] = hat
        normed[:, cols] = hat.astype(BF16)

    loads[10].wait()
    pre = dot(normed[...], win[...])
    preact[...] = pre
    hidden = (pre * jax.nn.sigmoid(pre)).astype(BF16)
    loads[11].wait()
    raw = dot(hidden, wout[...])
    norms = jnp.sqrt(jnp.sum(raw * raw, axis=1, keepdims=True) + 1e-06)
    unit32 = raw / norms
    units = unit32.astype(BF16)
    group[pl.ds(pl.multiple_of(blk * COUNT, COUNT), COUNT), :] = units
    gathered = to_group(group, COUNT)

    asked.wait_recv()
    pick32 = jnp.where(flat(ask_in) == lane.astype(F32), 1.0, 0.0)
    returned = spread(dot(pick32.astype(BF16), units), row_out, row_in)

    unpick = pick32.T.astype(BF16)
    base = core * (FEATS // 2)
    for k in range(8):
        cols = pl.ds(pl.multiple_of((1 - core) * (FEATS // 2) + k * FILTERS, FILTERS), FILTERS)
        nt_send[k * FILTERS : (k + 1) * FILTERS, :] = normed[:, cols].T
    factor = remote(nt_send, nt_sib, sibling)
    for k in range(8):
        cols = pl.ds(pl.multiple_of(base + k * FILTERS, FILTERS), FILTERS)
        nt_own[k * FILTERS : (k + 1) * FILTERS, :] = normed[:, cols].T

    gathered.wait_recv()
    keys = group[...]
    scores = SCALE * dot_t(units, keys)
    self_lane = blk * COUNT + iota((COUNT, GROUP), 0)
    expo = jnp.where(iota((COUNT, GROUP), 1) == self_lane, 0.0, jnp.exp(scores))
    zneg = jnp.sum(expo, axis=1, keepdims=True)
    numer = dot(expo.astype(BF16), keys)

    returned.wait_recv()
    positive = dot(from_slot, flat(row_in).astype(BF16))
    own = units.astype(F32)
    spos = SCALE * jnp.sum(own * positive, axis=1, keepdims=True)
    epos = jnp.exp(spos)
    totals = epos + zneg
    tot_lane = jnp.broadcast_to(totals, (COUNT, COUNT)).T
    tot_all[pl.ds(pl.multiple_of(blk * TILE, TILE), TILE), :] = tot_lane[:TILE]
    tots = to_group(tot_all, TILE)
    away = COEF * (epos / totals - 1.0)
    high, low = split(away * own)
    backs = spread(dot(to_slot, high) + dot(to_slot, low), back_out, back_in)
    spos_lane = jnp.broadcast_to(spos, (COUNT, COUNT)).T
    loss[...] = (jnp.log(tot_lane) - spos_lane)[:1]
    keep(loss, loss_ref)
    grad_units = away * positive + COEF * (numer / totals)
    hid_t[...] = hidden.T
    for k in range(2 * FREQS):
        spec_t[:, k * COUNT : (k + 1) * COUNT] = spec[k * COUNT : (k + 1) * COUNT, :].T

    tots.wait_recv()
    inverse = jnp.concatenate(
        [1.0 / tot_all[b * TILE : b * TILE + 1, :] for b in range(CYCLE)], axis=1
    )
    keyterm = dot((expo * inverse).astype(BF16), keys)
    grad_units = grad_units + COEF * keyterm
    backs.wait_recv()
    high, low = split(flat(back_in))
    grad_units = grad_units + (dot(unpick, high) + dot(unpick, low))

    grad_raw = (
        (grad_units - unit32 * jnp.sum(unit32 * grad_units, axis=1, keepdims=True)) / norms
    ).astype(BF16)
    grad_hid = dot_t(grad_raw, wout[...])
    pre = preact[...]
    sigm = jax.nn.sigmoid(pre)
    grad_pre = (grad_hid * sigm * (1.0 + pre * (1.0 - sigm))).astype(BF16)
    gp_own[...] = grad_pre
    sent = remote(gp_own, gp_sib, sibling)
    g_out = dot(hid_t[...], grad_raw)
    sm[0, 0:256, :] = g_out[:256]
    sm[1, 0:256, :] = g_out[256:]
    ngrad[...] = dot_t(grad_pre, win[...])

    factor.wait_recv()
    sent.wait_recv()
    right = jnp.concatenate([gp_own[...], gp_sib[...]], axis=0)
    def multiply(to, n):
        for i in range(2):
            rows = slice(n * 512 + i * 256, n * 512 + (i + 1) * 256)
            prod = dot(jnp.concatenate([nt_own[rows, :], nt_sib[rows, :]], axis=1), right)
            to[i * 256 : (i + 1) * 256, :] = prod.astype(BF16)

    xs = [lax.rem(x + k, 4) for k in range(4)]
    ys = [lax.rem(y + k, 4) for k in range(4)]
    zs = [lax.rem(z + k, 8) for k in range(8)]
    x_peers = [device(xs[k], y, z, core) for k in range(4)]
    y_peers = [device(x, ys[k], z, core) for k in range(4)]
    z_peers = [device(x, y, zs[k], core) for k in range(8)]

    def piece(at, rows):
        return pl.ds(pl.multiple_of(at * rows, rows), rows)

    parts = (
        (pa, ra1, pa2, ra2, xs, ys, x_peers, y_peers),
        (pb, rb1, pb2, rb2, ys, xs, y_peers, x_peers),
    )
    far4 = (2, 1, 3)
    far = (4, 3, 5, 2, 6, 1, 7)
    step1 = ({}, {})
    for n, (src, got, _, _, u, v, u_peer, _) in enumerate(parts):
        multiply(src, n)
        for j in (2, 1, 3, 0):
            for k in far4:
                step1[n][j, k] = remote(
                    src.at[piece(u[k] * 4 + v[j], 32)],
                    got.at[k - 1, piece(v[j], 32)],
                    u_peer[k],
                )

    acc = jnp.zeros((COUNT, FILTERS), F32)
    acc_hat = jnp.zeros((COUNT, FILTERS), F32)
    for k in range(FREQS):
        cols = slice(k * FILTERS, (k + 1) * FILTERS)
        ng = ngrad[:, cols]
        acc = acc + ng
        acc_hat = acc_hat + ng * feat[:, cols]
    mean_ng = jnp.sum(acc, axis=1, keepdims=True) * (1.0 / FEATS)
    mean_hat = jnp.sum(acc_hat, axis=1, keepdims=True) * (1.0 / FEATS)
    for k in range(FREQS):
        cols = slice(k * FILTERS, (k + 1) * FILTERS)
        rows = slice(k * COUNT, (k + 1) * COUNT)
        re = real[rows, :]
        im = imag[rows, :]
        grad_feat = rscale * (ngrad[:, cols] - mean_ng - feat[:, cols] * mean_hat)
        grad_pow = 2.0 * grad_feat / (1.0 + (re * re + im * im))
        mixg[rows, :] = (re * grad_pow).astype(BF16)
        mixg[(FREQS + k) * COUNT : (FREQS + k + 1) * COUNT, :] = (im * grad_pow).astype(BF16)
    g_mix = dot(spec_t[...], mixg[...])
    sm[0, 256:384, :] = g_mix[:128]
    sm[1, 256:384, :] = g_mix[128:]
    halves = remote(sm.at[other], sm_sib, sibling)

    def add(own_part, got, copies):
        value = own_part.astype(F32)
        for k in sorted(copies):
            copies[k].wait_recv()
            value = value + got[k - 1].astype(F32)
        return value.astype(BF16)

    step2 = ({}, {})
    for j in (2, 1, 3, 0):
        for n, (src, got, src2, got2, u, v, _, v_peer) in enumerate(parts):
            mine = piece(v[j], 32)
            value = src[piece(u[0] * 4 + v[j], 32), :].astype(F32)
            for k in (1, 3, 2):
                step1[n][j, k].wait_recv()
                value = value + got[k - 1, mine, :].astype(F32)
            src2[mine, :] = value.astype(BF16)
            if j:
                step2[n][j] = remote(src2.at[mine], got2.at[j - 1], v_peer[j])

    halves.wait_recv()
    sm0[...] = (sm[core] + sm_sib[...]).astype(BF16)
    s1 = {k: remote(sm0.at[piece(zs[k], 48)], sz.at[k - 1], z_peers[k]) for k in far}

    before_z = len(started)
    for n, (_, _, src2, got2, _, v, _, _) in enumerate(parts):
        value = add(src2[piece(v[0], 32), :], got2, step2[n])
        for at in range(8):
            cells[at, n * 16 : n * 16 + 16, :] = value[
                at // 4 * 16 : at // 4 * 16 + 16, at % 4 * 128 : at % 4 * 128 + 128
            ]
    step3 = {k: remote(cells.at[zs[k]], cells_in.at[k - 1], z_peers[k]) for k in far}

    sx[x] = add(sm0[piece(z, 48), :], sz, s1)
    s2 = [remote(sx.at[x], sx.at[x], x_peers[k]) for k in far4]

    def place(c, n, u, v, rows):
        return pl.ds(pl.multiple_of(c * 1024 + n * 512 + u * 128 + v * 32, 32), rows)

    done[z] = add(cells[z], cells_in, step3)
    step4 = [remote(done.at[z], done.at[z], z_peers[k]) for k in far]

    def four(ref):
        value = ref[0].astype(F32)
        for i in range(1, 4):
            value = value + ref[i].astype(F32)
        return value.astype(BF16)

    settle(before_z)
    for copy in s2:
        copy.wait_recv()
    sy[y] = four(sx)
    s3 = [remote(sy.at[y], sy.at[y], y_peers[k]) for k in far4]

    before_gather = len(started) - 3
    step5 = ({}, {})
    step6 = ({}, {})

    def forward(n, m):
        u, v, u_peer = parts[n][4], parts[n][5], parts[n][6]
        block = big.at[place(core, n, u[0], v[(4 - m) % 4], 32)]
        for k in far4:
            step6[n][m, k] = remote(block, block, u_peer[k])

    for copy in step4:
        copy.wait_recv()
    for n in range(2):
        u, v, v_peer = parts[n][4], parts[n][5], parts[n][7]
        for at in range(8):
            rows = pl.ds(pl.multiple_of(core * 1024 + n * 512 + u[0] * 128 + v[0] * 32 + at // 4 * 16, 16), 16)
            big[rows, at % 4 * 128 : at % 4 * 128 + 128] = done[at, n * 16 : n * 16 + 16, :]
        block = big.at[place(core, n, u[0], v[0], 32)]
        for k in far4:
            step5[n][k] = remote(block, block, v_peer[k])
    for n in range(2):
        forward(n, 0)

    for copy in s3:
        copy.wait_recv()
    small[core, piece(z, 48), :] = four(sy)
    bit = small.at[core, piece(z, 48)]
    s4 = [remote(bit, bit, z_peers[k]) for k in far]

    for m in (1, 3, 2):
        for n in range(2):
            step5[n][m].wait_recv()
            forward(n, m)

    last = []

    def cross(n, u):
        chunk = place(core, n, u, 0, 128)
        last.append(remote(big.at[chunk], big_ref.at[chunk], sibling))
        keep(big.at[chunk], big_ref.at[chunk])

    for n in range(2):
        cross(n, parts[n][4][0])
    settle(before_gather)
    for copy in s4:
        copy.wait_recv()
    last.append(remote(small.at[core], small_ref.at[core], sibling))
    keep(small.at[core], small_ref.at[core])
    before_last = len(started)
    for k in (1, 3, 2):
        if k == 2:
            settle(before_last)
        for n in range(2):
            for m in (0, 1, 3, 2):
                step6[n][m, k].wait_recv()
            cross(n, parts[n][4][4 - k])
    for copy in last:
        copy.wait_recv()
    settle(len(started))
    for copy in kept:
        copy.wait()


N_SEM = 160
N_KEEP = 24


STEPS = 8


def widen(big_ref, small_ref, loss_ref, in_ref, out_ref, mix_ref, rows_ref, big, wide, small, small32, load_sem, store_sem):
    size = FEATS // STEPS
    loads = []
    stores = [pltpu.make_async_copy(loss_ref, rows_ref, store_sem.at[STEPS])]
    stores[0].start()
    for i in range(STEPS):
        rows = pl.ds(i * size, size)
        loads.append(pltpu.make_async_copy(big_ref.at[rows], big.at[rows], load_sem.at[i]))
    loads.append(pltpu.make_async_copy(small_ref, small, load_sem.at[STEPS]))
    for load in loads:
        load.start()
    for i in range(STEPS):
        rows = pl.ds(i * size, size)
        loads[i].wait()
        wide[rows, :] = big[rows, :].astype(F32)
        stores.append(pltpu.make_async_copy(wide.at[rows], in_ref.at[rows], store_sem.at[i]))
        stores[-1].start()
    loads[STEPS].wait()
    small32[...] = small[...].astype(F32)
    for h in range(2):
        at = small32.at[h, pl.ds(0, 256)]
        stores.append(pltpu.make_async_copy(at, out_ref.at[pl.ds(h * 256, 256)], store_sem.at[STEPS + 1 + h]))
        stores[-1].start()
        at = small32.at[h, pl.ds(256, 128)]
        stores.append(pltpu.make_async_copy(at, mix_ref.at[pl.ds(h * 128, 128)], store_sem.at[STEPS + 3 + h]))
        stores[-1].start()
    for store in stores:
        store.wait()


def on_device(patches, w_mix, w_in, w_out, partner_dev, partner_row):
    vmem = pltpu.VMEM
    any_spec = pl.BlockSpec(memory_space=pl.ANY)
    scratch = [
        vmem((1, COUNT), jnp.int32),
        vmem((1, COUNT), jnp.int32),
        vmem((COUNT * ANGLES, LANES), BF16),
        vmem((128, 256), BF16),
        vmem((LANES, FILTERS), BF16),
        vmem((FEATS, HIDDEN), BF16),
        vmem((HIDDEN, EMBED), BF16),
        vmem((2 * FREQS * COUNT, LANES), BF16),
        vmem((LANES, 2 * FREQS * COUNT), BF16),
        vmem((FREQS * COUNT, FILTERS), F32),
        vmem((FREQS * COUNT, FILTERS), F32),
        vmem((COUNT, FEATS), F32),
        vmem((COUNT, FEATS), BF16),
        vmem((COUNT, HIDDEN), F32),
        vmem((HIDDEN, COUNT), BF16),
        vmem((COUNT, FEATS), F32),
        vmem((2 * FREQS * COUNT, FILTERS), BF16),
        vmem((GROUP, EMBED), BF16),
        vmem((PEERS, SLOT, COUNT), F32),
        vmem((PEERS, SLOT, COUNT), F32),
        vmem((PEERS, SLOT, COUNT), F32),
        vmem((PEERS, SLOT, COUNT), F32),
        vmem((PEERS, SLOT, COUNT), F32),
        vmem((PEERS, SLOT, COUNT), F32),
        vmem((CYCLE * TILE, COUNT), F32),
        vmem((FEATS // 2, COUNT), BF16),
        vmem((FEATS // 2, COUNT), BF16),
        vmem((FEATS // 2, COUNT), BF16),
        vmem((COUNT, HIDDEN), BF16),
        vmem((COUNT, HIDDEN), BF16),
        vmem((512, 512), BF16),
        vmem((512, 512), BF16),
        vmem((3, 128, 512), BF16),
        vmem((3, 128, 512), BF16),
        vmem((128, 512), BF16),
        vmem((128, 512), BF16),
        vmem((3, 32, 512), BF16),
        vmem((3, 32, 512), BF16),
        vmem((8, 32, 128), BF16),
        vmem((7, 32, 128), BF16),
        vmem((8, 32, 128), BF16),
        vmem((2, SMALL, 128), F32),
        vmem((SMALL, 128), F32),
        vmem((SMALL, 128), BF16),
        vmem((7, 48, 128), BF16),
        vmem((4, 48, 128), BF16),
        vmem((4, 48, 128), BF16),
        vmem((FEATS, HIDDEN), BF16),
        vmem((2, SMALL, 128), BF16),
        vmem((1, COUNT), F32),
        pltpu.SemaphoreType.DMA((14,)),
        pltpu.SemaphoreType.DMA((N_KEEP,)),
        pltpu.SemaphoreType.DMA((N_SEM,)),
        pltpu.SemaphoreType.DMA((N_SEM,)),
    ]
    loss, big, small = pl.pallas_call(
        kernel,
        name="contrastive_step",
        out_shape=(
            jax.ShapeDtypeStruct((1, COUNT), F32),
            jax.ShapeDtypeStruct((FEATS, HIDDEN), BF16),
            jax.ShapeDtypeStruct((2, SMALL, 128), BF16),
        ),
        in_specs=[any_spec] * 7,
        out_specs=(any_spec, any_spec, any_spec),
        scratch_shapes=scratch,
        compiler_params=pltpu.CompilerParams(
            collective_id=0, has_side_effects=True, vmem_limit_bytes=56 * 2**20
        ),
    )(
        partner_dev.reshape(1, COUNT),
        partner_row.reshape(1, COUNT),
        jnp.asarray(block_table()),
        w_mix,
        w_in,
        w_out,
        patches.reshape(COUNT * ANGLES, LANES),
    )
    g_in, g_out, g_mix, loss = pl.pallas_call(
        widen,
        name="widen",
        out_shape=(
            jax.ShapeDtypeStruct((FEATS, HIDDEN), F32),
            jax.ShapeDtypeStruct((HIDDEN, EMBED), F32),
            jax.ShapeDtypeStruct((LANES, FILTERS), F32),
            jax.ShapeDtypeStruct((1, COUNT), F32),
        ),
        in_specs=[any_spec] * 3,
        out_specs=(any_spec,) * 4,
        scratch_shapes=[
            vmem((FEATS, HIDDEN), BF16),
            vmem((FEATS, HIDDEN), F32),
            vmem((2, SMALL, 128), BF16),
            vmem((2, SMALL, 128), F32),
            pltpu.SemaphoreType.DMA((STEPS + 1,)),
            pltpu.SemaphoreType.DMA((STEPS + 5,)),
        ],
        compiler_params=pltpu.CompilerParams(vmem_limit_bytes=56 * 2**20),
    )(big, small, loss)
    return (loss.reshape(COUNT), g_mix, g_in, g_out)


def solution(mesh):
    placed = (P(("blk", "dp"), None, None), P(), P(), P(), P(("blk", "dp")), P(("blk", "dp")))
    return jax.shard_map(
        on_device,
        mesh=mesh,
        in_specs=placed,
        out_specs=(P(("blk", "dp")), P(), P(), P()),
        check_vma=False,
    )
```

```python
import functools
import math

import jax
import jax.numpy as jnp
import ml_dtypes
import numpy as np
from jax import lax
from jax.experimental import pallas as pl
from jax.experimental.pallas import tpu as pltpu
from jax.sharding import PartitionSpec as P

SCALE = 10.0
MESH = pl.DeviceIdType.MESH
F32 = jnp.float32
BF16 = jnp.bfloat16

COUNT = 128
ANGLES = 64
LANES = 256
FREQS = 16
FILTERS = 128
FEATS = FREQS * FILTERS
HIDDEN = 512
EMBED = 128
PEERS = 32
CYCLE = 8
GROUP = CYCLE * COUNT
SLOT = COUNT // PEERS
TILE = 8
SMALL = 384
COEF = SCALE / COUNT


def block_table():
    angle = np.arange(ANGLES)
    freq = np.arange(FREQS)
    phase = np.mod(freq[None, :] * angle[:, None], ANGLES).astype(np.float32) * np.float32(
        2.0 * math.pi / ANGLES
    )
    table = np.concatenate([np.cos(phase), -np.sin(phase)], axis=1)
    wide = np.zeros((2 * FREQS, 4, 4, ANGLES), np.float32)
    for n in range(4):
        wide[:, n, n, :] = table.T
    return wide.reshape(2 * FREQS * 4, 4 * ANGLES).astype(ml_dtypes.bfloat16)


def dot(a, b):
    return jnp.dot(a, b, preferred_element_type=F32)


def dot_t(a, b):
    return lax.dot_general(a, b, (((1,), (1,)), ((), ())), preferred_element_type=F32)


def split(v):
    high = v.astype(BF16)
    return high, (v - high.astype(F32)).astype(BF16)


def iota(shape, dim):
    return lax.broadcasted_iota(jnp.int32, shape, dim)


def kernel(
    pdev_hbm, prow_hbm, table_hbm, wmix_hbm, win_hbm, wout_hbm, patches_hbm,
    loss_ref, big_ref, small_ref,
    pdev_ref, prow_ref, patches, table, wmix, win, wout,
    spec, spec_t, real, imag, feat, normed, preact, hid_t, ngrad, mixg,
    group, ask_out, ask_in, row_out, row_in, back_out, back_in, tot_all,
    nt_own, nt_send, nt_sib, gp_own, gp_sib,
    pa, pb, ra1, rb1, pa2, pb2, ra2, rb2, pa3, pb3, ra3, rb3,
    sm, sm_sib, sm0, sz, sx, sy,
    big, small, loss,
    load_sem, keep_sem, send_sem, recv_sem,
):
    blk = lax.axis_index("blk")
    dp = lax.axis_index("dp")
    y = lax.div(blk, 2)
    x_low = lax.div(dp, 16)
    x = lax.rem(blk, 2) * 2 + x_low
    z = lax.rem(lax.div(dp, 2), 8)
    core = lax.rem(dp, 2)
    other = 1 - core

    def device(x_, y_, z_, c_):
        return (y_ * 2 + lax.div(x_, 2), lax.rem(x_, 2) * 16 + z_ * 2 + c_)

    sibling = device(x, y, z, other)

    dp_peers = []
    for dz in (4, 5, 3, 6, 2, 7, 1, 0):
        z_part = lax.rem(z + dz, 8) * 2
        for x_part in ((1 - x_low) * 16, x_low * 16):
            for c_part in (other, core):
                dp_peers.append(x_part + z_part + c_part)
    dp_peers = dp_peers[:-1]
    blk_peers = [lax.rem(blk + step, CYCLE) for step in (5, 4, 3, 2, 1, 6, 7)]

    used = [0]
    started = []

    def remote(src, dst, to):
        k = used[0]
        used[0] += 1
        copy = pltpu.make_async_remote_copy(
            src_ref=src, dst_ref=dst, send_sem=send_sem.at[k], recv_sem=recv_sem.at[k],
            device_id=to, device_id_type=MESH,
        )
        copy.start()
        started.append(copy)
        return copy

    def spread(value, src, dst):
        k = used[0]
        used[0] += 1
        for p in range(PEERS):
            src[p] = value[p * SLOT : (p + 1) * SLOT]

        for p in dp_peers:
            pltpu.make_async_remote_copy(
                src_ref=src.at[p], dst_ref=dst.at[dp],
                send_sem=send_sem.at[k], recv_sem=recv_sem.at[k],
                device_id=(blk, p), device_id_type=MESH,
            ).start()
        dst[dp] = src[dp]
        rows = pl.ds(0, PEERS - 1)
        whole = pltpu.make_async_remote_copy(
            src_ref=src.at[rows], dst_ref=dst.at[rows], send_sem=send_sem.at[k],
            recv_sem=recv_sem.at[k], device_id=(blk, dp_peers[0]), device_id_type=MESH,
        )
        started.append(whole)
        return whole

    def flat(ref):
        return jnp.concatenate([ref[p] for p in range(PEERS)], axis=0)

    def to_group(ref, rows):
        k = used[0]
        used[0] += 1
        mine = pl.ds(pl.multiple_of(blk * rows, rows), rows)
        for b in blk_peers:
            pltpu.make_async_remote_copy(
                src_ref=ref.at[mine], dst_ref=ref.at[mine],
                send_sem=send_sem.at[k], recv_sem=recv_sem.at[k],
                device_id=(b, dp), device_id_type=MESH,
            ).start()
        span = pl.ds(0, (CYCLE - 1) * rows)
        whole = pltpu.make_async_remote_copy(
            src_ref=ref.at[span], dst_ref=ref.at[span], send_sem=send_sem.at[k],
            recv_sem=recv_sem.at[k], device_id=(blk_peers[0], dp), device_id_type=MESH,
        )
        started.append(whole)
        return whole

    kept = []

    def keep(src, dst):
        copy = pltpu.make_async_copy(src, dst, keep_sem.at[len(kept)])
        copy.start()
        kept.append(copy)

    barrier = pltpu.get_barrier_semaphore()

    for p in dp_peers:
        pl.semaphore_signal(barrier, inc=1, device_id=(blk, p), device_id_type=MESH)
    for b in blk_peers:
        pl.semaphore_signal(barrier, inc=1, device_id=(b, dp), device_id_type=MESH)
    pl.semaphore_signal(barrier, inc=1, device_id=device(3 - x, y, z, core), device_id_type=MESH)

    chunk = 1024
    loads = [pltpu.make_async_copy(table_hbm, table, load_sem.at[0])]
    for g in range(8):
        rows = pl.ds(g * chunk, chunk)
        loads.append(pltpu.make_async_copy(patches_hbm.at[rows], patches.at[rows], load_sem.at[1 + g]))
    loads.append(pltpu.make_async_copy(wmix_hbm, wmix, load_sem.at[9]))
    loads.append(pltpu.make_async_copy(win_hbm, win, load_sem.at[10]))
    loads.append(pltpu.make_async_copy(wout_hbm, wout, load_sem.at[11]))
    loads.append(pltpu.make_async_copy(pdev_hbm, pdev_ref, load_sem.at[12]))
    loads.append(pltpu.make_async_copy(prow_hbm, prow_ref, load_sem.at[13]))
    for i in (12, 13) + tuple(range(12)):
        loads[i].start()

    loads[12].wait()
    loads[13].wait()
    lane = iota((COUNT, COUNT), 1)
    row = iota((COUNT, COUNT), 0)
    dev_lane = jnp.broadcast_to(pdev_ref[...], (COUNT, COUNT))
    dev_row = dev_lane.astype(F32).T.astype(jnp.int32)
    same = dev_lane == dev_row
    rank_lane = jnp.sum(jnp.where(same & (row < lane), 1.0, 0.0), axis=0, keepdims=True)
    rank_row = jnp.sum(jnp.where(same & (lane < row), 1.0, 0.0), axis=1, keepdims=True)
    place_lane = pdev_ref[...] * SLOT + rank_lane.astype(jnp.int32)
    place_row = dev_row[:, :1] * SLOT + rank_row.astype(jnp.int32)
    to_slot = jnp.where(
        iota((PEERS * SLOT, COUNT), 0) == place_lane, 1.0, 0.0
    ).astype(BF16)
    from_slot = jnp.where(
        iota((COUNT, PEERS * SLOT), 1) == place_row, 1.0, 0.0
    ).astype(BF16)
    prow = jnp.broadcast_to(prow_ref[...], (COUNT, COUNT)).astype(F32).T.astype(BF16)
    ask = dot(to_slot, prow)

    loads[0].wait()
    bank = table[...]
    for g in range(8):
        loads[1 + g].wait()
        quads = [dot(bank, patches[g * chunk + q * 256 : g * chunk + (q + 1) * 256, :]) for q in range(4)]
        for k in range(2 * FREQS):
            part = jnp.concatenate([quad[k * 4 : k * 4 + 4] for quad in quads], axis=0)
            spec[k * COUNT + g * 16 : k * COUNT + g * 16 + 16, :] = part.astype(BF16)
        if g == 2:
            pl.semaphore_wait(barrier, PEERS - 1 + CYCLE - 1 + 1)
            asked = spread(ask, ask_out, ask_in)

    loads[9].wait()
    total = jnp.zeros((COUNT, 1), F32)
    for k in range(0, FREQS, 4):
        rows = slice(k * COUNT, (k + 4) * COUNT)
        re = dot(spec[rows, :], wmix[...])
        im = dot(spec[(FREQS + k) * COUNT : (FREQS + k + 4) * COUNT, :], wmix[...])
        real[rows, :] = re
        imag[rows, :] = im
        value = jnp.log1p(re * re + im * im)
        acc = jnp.zeros((COUNT, FILTERS), F32)
        for i in range(4):
            piece = value[i * COUNT : (i + 1) * COUNT]
            feat[:, (k + i) * FILTERS : (k + i + 1) * FILTERS] = piece
            acc = acc + piece
        total = total + jnp.sum(acc, axis=1, keepdims=True)
    mean = total * (1.0 / FEATS)
    acc = jnp.zeros((COUNT, FILTERS), F32)
    for k in range(FREQS):
        off = feat[:, k * FILTERS : (k + 1) * FILTERS] - mean
        acc = acc + off * off
    rscale = lax.rsqrt(jnp.sum(acc, axis=1, keepdims=True) * (1.0 / FEATS) + 1e-05)
    for k in range(FREQS):
        cols = slice(k * FILTERS, (k + 1) * FILTERS)
        hat = (feat[:, cols] - mean) * rscale
        feat[:, cols] = hat
        normed[:, cols] = hat.astype(BF16)

    loads[10].wait()
    pre = dot(normed[...], win[...])
    preact[...] = pre
    hidden = (pre * jax.nn.sigmoid(pre)).astype(BF16)
    loads[11].wait()
    raw = dot(hidden, wout[...])
    norms = jnp.sqrt(jnp.sum(raw * raw, axis=1, keepdims=True) + 1e-06)
    unit32 = raw / norms
    units = unit32.astype(BF16)
    group[pl.ds(pl.multiple_of(blk * COUNT, COUNT), COUNT), :] = units
    gathered = to_group(group, COUNT)

    asked.wait_recv()
    pick32 = jnp.where(flat(ask_in) == lane.astype(F32), 1.0, 0.0)
    returned = spread(dot(pick32.astype(BF16), units), row_out, row_in)

    unpick = pick32.T.astype(BF16)
    base = core * (FEATS // 2)
    for k in range(8):
        cols = pl.ds(pl.multiple_of((1 - core) * (FEATS // 2) + k * FILTERS, FILTERS), FILTERS)
        nt_send[k * FILTERS : (k + 1) * FILTERS, :] = normed[:, cols].T
    factor = remote(nt_send, nt_sib, sibling)
    for k in range(8):
        cols = pl.ds(pl.multiple_of(base + k * FILTERS, FILTERS), FILTERS)
        nt_own[k * FILTERS : (k + 1) * FILTERS, :] = normed[:, cols].T

    gathered.wait_recv()
    keys = group[...]
    scores = SCALE * dot_t(units, keys)
    self_lane = blk * COUNT + iota((COUNT, GROUP), 0)
    expo = jnp.where(iota((COUNT, GROUP), 1) == self_lane, 0.0, jnp.exp(scores))
    zneg = jnp.sum(expo, axis=1, keepdims=True)
    numer = dot(expo.astype(BF16), keys)

    returned.wait_recv()
    positive = dot(from_slot, flat(row_in).astype(BF16))
    own = units.astype(F32)
    spos = SCALE * jnp.sum(own * positive, axis=1, keepdims=True)
    epos = jnp.exp(spos)
    totals = epos + zneg
    tot_lane = jnp.broadcast_to(totals, (COUNT, COUNT)).T
    tot_all[pl.ds(pl.multiple_of(blk * TILE, TILE), TILE), :] = tot_lane[:TILE]
    tots = to_group(tot_all, TILE)
    away = COEF * (epos / totals - 1.0)
    high, low = split(away * own)
    backs = spread(dot(to_slot, high) + dot(to_slot, low), back_out, back_in)
    spos_lane = jnp.broadcast_to(spos, (COUNT, COUNT)).T
    loss[...] = (jnp.log(tot_lane) - spos_lane)[:1]
    keep(loss, loss_ref)
    grad_units = away * positive + COEF * (numer / totals)
    hid_t[...] = hidden.T
    for k in range(2 * FREQS):
        spec_t[:, k * COUNT : (k + 1) * COUNT] = spec[k * COUNT : (k + 1) * COUNT, :].T

    tots.wait_recv()
    inverse = jnp.concatenate(
        [1.0 / tot_all[b * TILE : b * TILE + 1, :] for b in range(CYCLE)], axis=1
    )
    keyterm = dot((expo * inverse).astype(BF16), keys)
    grad_units = grad_units + COEF * keyterm
    backs.wait_recv()
    high, low = split(flat(back_in))
    grad_units = grad_units + (dot(unpick, high) + dot(unpick, low))

    grad_raw = (
        (grad_units - unit32 * jnp.sum(unit32 * grad_units, axis=1, keepdims=True)) / norms
    ).astype(BF16)
    grad_hid = dot_t(grad_raw, wout[...])
    pre = preact[...]
    sigm = jax.nn.sigmoid(pre)
    grad_pre = (grad_hid * sigm * (1.0 + pre * (1.0 - sigm))).astype(BF16)
    gp_own[...] = grad_pre
    sent = remote(gp_own, gp_sib, sibling)
    g_out = dot(hid_t[...], grad_raw)
    sm[0, 0:256, :] = g_out[:256]
    sm[1, 0:256, :] = g_out[256:]
    ngrad[...] = dot_t(grad_pre, win[...])

    factor.wait_recv()
    sent.wait_recv()
    right = jnp.concatenate([gp_own[...], gp_sib[...]], axis=0)
    def multiply(to, n):
        for i in range(2):
            rows = slice(n * 512 + i * 256, n * 512 + (i + 1) * 256)
            prod = dot(jnp.concatenate([nt_own[rows, :], nt_sib[rows, :]], axis=1), right)
            to[i * 256 : (i + 1) * 256, :] = prod.astype(BF16)

    xs = [lax.rem(x + k, 4) for k in range(4)]
    ys = [lax.rem(y + k, 4) for k in range(4)]
    zs = [lax.rem(z + k, 8) for k in range(8)]
    x_peers = [device(xs[k], y, z, core) for k in range(4)]
    y_peers = [device(x, ys[k], z, core) for k in range(4)]
    z_peers = [device(x, y, zs[k], core) for k in range(8)]

    def piece(at, rows):
        return pl.ds(pl.multiple_of(at * rows, rows), rows)

    def cell(at):
        return (piece(lax.div(at, 4), 16), piece(lax.rem(at, 4), 128))

    parts = (
        (pa, ra1, pa2, ra2, pa3, ra3, xs, ys, x_peers, y_peers),
        (pb, rb1, pb2, rb2, pb3, rb3, ys, xs, y_peers, x_peers),
    )
    far4 = (2, 1, 3)
    far = (4, 3, 5, 2, 6, 1, 7)
    step1 = ({}, {})
    for n, (src, got, _, _, _, _, u, v, u_peer, _) in enumerate(parts):
        multiply(src, n)
        for j in (2, 1, 3, 0):
            for k in far4:
                step1[n][j, k] = remote(
                    src.at[piece(u[k] * 4 + v[j], 32)],
                    got.at[k - 1, piece(v[j], 32)],
                    u_peer[k],
                )

    acc = jnp.zeros((COUNT, FILTERS), F32)
    acc_hat = jnp.zeros((COUNT, FILTERS), F32)
    for k in range(FREQS):
        cols = slice(k * FILTERS, (k + 1) * FILTERS)
        ng = ngrad[:, cols]
        acc = acc + ng
        acc_hat = acc_hat + ng * feat[:, cols]
    mean_ng = jnp.sum(acc, axis=1, keepdims=True) * (1.0 / FEATS)
    mean_hat = jnp.sum(acc_hat, axis=1, keepdims=True) * (1.0 / FEATS)
    for k in range(FREQS):
        cols = slice(k * FILTERS, (k + 1) * FILTERS)
        rows = slice(k * COUNT, (k + 1) * COUNT)
        re = real[rows, :]
        im = imag[rows, :]
        grad_feat = rscale * (ngrad[:, cols] - mean_ng - feat[:, cols] * mean_hat)
        grad_pow = 2.0 * grad_feat / (1.0 + (re * re + im * im))
        mixg[rows, :] = (re * grad_pow).astype(BF16)
        mixg[(FREQS + k) * COUNT : (FREQS + k + 1) * COUNT, :] = (im * grad_pow).astype(BF16)
    g_mix = dot(spec_t[...], mixg[...])
    sm[0, 256:384, :] = g_mix[:128]
    sm[1, 256:384, :] = g_mix[128:]
    halves = remote(sm.at[other], sm_sib, sibling)

    def add(own_part, got, copies):
        value = own_part.astype(F32)
        for k in sorted(copies):
            copies[k].wait_recv()
            value = value + got[k - 1].astype(F32)
        return value.astype(BF16)

    step2 = ({}, {})
    for j in (2, 1, 3, 0):
        for n, (src, got, src2, got2, _, _, u, v, _, v_peer) in enumerate(parts):
            mine = piece(v[j], 32)
            value = src[piece(u[0] * 4 + v[j], 32), :].astype(F32)
            for k in (1, 3, 2):
                step1[n][j, k].wait_recv()
                value = value + got[k - 1, mine, :].astype(F32)
            src2[mine, :] = value.astype(BF16)
            if j:
                step2[n][j] = remote(src2.at[mine], got2.at[j - 1], v_peer[j])

    halves.wait_recv()
    sm0[...] = (sm[core] + sm_sib[...]).astype(BF16)
    s1 = {k: remote(sm0.at[piece(zs[k], 48)], sz.at[k - 1], z_peers[k]) for k in far}

    step3 = ({}, {})
    for n, (_, _, src2, got2, src3, got3, _, v, _, _) in enumerate(parts):
        src3[...] = add(src2[piece(v[0], 32), :], got2, step2[n])
        for k in far:
            step3[n][k] = remote(src3.at[cell(zs[k])], got3.at[k - 1], z_peers[k])

    sx[x] = add(sm0[piece(z, 48), :], sz, s1)
    s2 = [remote(sx.at[x], sx.at[x], x_peers[k]) for k in far4]

    def place(c, n, u, v, rows):
        return pl.ds(pl.multiple_of(c * 1024 + n * 512 + u * 128 + v * 32, 32), rows)

    step4 = ([], [])
    for n, (_, _, _, _, src3, got3, u, v, _, _) in enumerate(parts):
        block = big.at[place(core, n, u[0], v[0], 32)]
        block[cell(z)] = add(src3[cell(z)], got3, step3[n])
        for k in far:
            here = block.at[cell(z)]
            step4[n].append(remote(here, here, z_peers[k]))

    def four(ref):
        value = ref[0].astype(F32)
        for i in range(1, 4):
            value = value + ref[i].astype(F32)
        return value.astype(BF16)

    for copy in s2:
        copy.wait_recv()
    sy[y] = four(sx)
    s3 = [remote(sy.at[y], sy.at[y], y_peers[k]) for k in far4]

    step5 = ({}, {})
    step6 = ({}, {})

    def forward(n, m):
        u, v, u_peer = parts[n][6], parts[n][7], parts[n][8]
        block = big.at[place(core, n, u[0], v[(4 - m) % 4], 32)]
        for k in far4:
            step6[n][m, k] = remote(block, block, u_peer[k])

    for n in range(2):
        u, v, v_peer = parts[n][6], parts[n][7], parts[n][9]
        for copy in step4[n]:
            copy.wait_recv()
        block = big.at[place(core, n, u[0], v[0], 32)]
        for k in far4:
            step5[n][k] = remote(block, block, v_peer[k])
    for n in range(2):
        forward(n, 0)

    for copy in s3:
        copy.wait_recv()
    small[core, piece(z, 48), :] = four(sy)
    bit = small.at[core, piece(z, 48)]
    s4 = [remote(bit, bit, z_peers[k]) for k in far]

    for m in (1, 3, 2):
        for n in range(2):
            step5[n][m].wait_recv()
            forward(n, m)

    last = []

    def cross(n, u):
        chunk = place(core, n, u, 0, 128)
        last.append(remote(big.at[chunk], big_ref.at[chunk], sibling))
        keep(big.at[chunk], big_ref.at[chunk])

    for n in range(2):
        cross(n, parts[n][6][0])
    for copy in s4:
        copy.wait_recv()
    last.append(remote(small.at[core], small_ref.at[core], sibling))
    keep(small.at[core], small_ref.at[core])
    for k in (1, 3, 2):
        for n in range(2):
            for m in (0, 1, 3, 2):
                step6[n][m, k].wait_recv()
            cross(n, parts[n][6][4 - k])
    for copy in last:
        copy.wait_recv()
    for copy in started:
        copy.wait_send()
    for copy in kept:
        copy.wait()


N_SEM = 160
N_KEEP = 24


STEPS = 8


def widen(big_ref, small_ref, loss_ref, in_ref, out_ref, mix_ref, rows_ref, big, wide, small, small32, load_sem, store_sem):
    size = FEATS // STEPS
    loads = []
    stores = [pltpu.make_async_copy(loss_ref, rows_ref, store_sem.at[STEPS])]
    stores[0].start()
    for i in range(STEPS):
        rows = pl.ds(i * size, size)
        loads.append(pltpu.make_async_copy(big_ref.at[rows], big.at[rows], load_sem.at[i]))
    loads.append(pltpu.make_async_copy(small_ref, small, load_sem.at[STEPS]))
    for load in loads:
        load.start()
    for i in range(STEPS):
        rows = pl.ds(i * size, size)
        loads[i].wait()
        wide[rows, :] = big[rows, :].astype(F32)
        stores.append(pltpu.make_async_copy(wide.at[rows], in_ref.at[rows], store_sem.at[i]))
        stores[-1].start()
    loads[STEPS].wait()
    small32[...] = small[...].astype(F32)
    for h in range(2):
        at = small32.at[h, pl.ds(0, 256)]
        stores.append(pltpu.make_async_copy(at, out_ref.at[pl.ds(h * 256, 256)], store_sem.at[STEPS + 1 + h]))
        stores[-1].start()
        at = small32.at[h, pl.ds(256, 128)]
        stores.append(pltpu.make_async_copy(at, mix_ref.at[pl.ds(h * 128, 128)], store_sem.at[STEPS + 3 + h]))
        stores[-1].start()
    for store in stores:
        store.wait()


def on_device(patches, w_mix, w_in, w_out, partner_dev, partner_row):
    vmem = pltpu.VMEM
    any_spec = pl.BlockSpec(memory_space=pl.ANY)
    scratch = [
        vmem((1, COUNT), jnp.int32),
        vmem((1, COUNT), jnp.int32),
        vmem((COUNT * ANGLES, LANES), BF16),
        vmem((128, 256), BF16),
        vmem((LANES, FILTERS), BF16),
        vmem((FEATS, HIDDEN), BF16),
        vmem((HIDDEN, EMBED), BF16),
        vmem((2 * FREQS * COUNT, LANES), BF16),
        vmem((LANES, 2 * FREQS * COUNT), BF16),
        vmem((FREQS * COUNT, FILTERS), F32),
        vmem((FREQS * COUNT, FILTERS), F32),
        vmem((COUNT, FEATS), F32),
        vmem((COUNT, FEATS), BF16),
        vmem((COUNT, HIDDEN), F32),
        vmem((HIDDEN, COUNT), BF16),
        vmem((COUNT, FEATS), F32),
        vmem((2 * FREQS * COUNT, FILTERS), BF16),
        vmem((GROUP, EMBED), BF16),
        vmem((PEERS, SLOT, COUNT), F32),
        vmem((PEERS, SLOT, COUNT), F32),
        vmem((PEERS, SLOT, COUNT), F32),
        vmem((PEERS, SLOT, COUNT), F32),
        vmem((PEERS, SLOT, COUNT), F32),
        vmem((PEERS, SLOT, COUNT), F32),
        vmem((CYCLE * TILE, COUNT), F32),
        vmem((FEATS // 2, COUNT), BF16),
        vmem((FEATS // 2, COUNT), BF16),
        vmem((FEATS // 2, COUNT), BF16),
        vmem((COUNT, HIDDEN), BF16),
        vmem((COUNT, HIDDEN), BF16),
        vmem((512, 512), BF16),
        vmem((512, 512), BF16),
        vmem((3, 128, 512), BF16),
        vmem((3, 128, 512), BF16),
        vmem((128, 512), BF16),
        vmem((128, 512), BF16),
        vmem((3, 32, 512), BF16),
        vmem((3, 32, 512), BF16),
        vmem((32, 512), BF16),
        vmem((32, 512), BF16),
        vmem((7, 16, 128), BF16),
        vmem((7, 16, 128), BF16),
        vmem((2, SMALL, 128), F32),
        vmem((SMALL, 128), F32),
        vmem((SMALL, 128), BF16),
        vmem((7, 48, 128), BF16),
        vmem((4, 48, 128), BF16),
        vmem((4, 48, 128), BF16),
        vmem((FEATS, HIDDEN), BF16),
        vmem((2, SMALL, 128), BF16),
        vmem((1, COUNT), F32),
        pltpu.SemaphoreType.DMA((14,)),
        pltpu.SemaphoreType.DMA((N_KEEP,)),
        pltpu.SemaphoreType.DMA((N_SEM,)),
        pltpu.SemaphoreType.DMA((N_SEM,)),
    ]
    loss, big, small = pl.pallas_call(
        kernel,
        name="contrastive_step",
        out_shape=(
            jax.ShapeDtypeStruct((1, COUNT), F32),
            jax.ShapeDtypeStruct((FEATS, HIDDEN), BF16),
            jax.ShapeDtypeStruct((2, SMALL, 128), BF16),
        ),
        in_specs=[any_spec] * 7,
        out_specs=(any_spec, any_spec, any_spec),
        scratch_shapes=scratch,
        compiler_params=pltpu.CompilerParams(
            collective_id=0, has_side_effects=True, vmem_limit_bytes=56 * 2**20
        ),
    )(
        partner_dev.reshape(1, COUNT),
        partner_row.reshape(1, COUNT),
        jnp.asarray(block_table()),
        w_mix,
        w_in,
        w_out,
        patches.reshape(COUNT * ANGLES, LANES),
    )
    g_in, g_out, g_mix, loss = pl.pallas_call(
        widen,
        name="widen",
        out_shape=(
            jax.ShapeDtypeStruct((FEATS, HIDDEN), F32),
            jax.ShapeDtypeStruct((HIDDEN, EMBED), F32),
            jax.ShapeDtypeStruct((LANES, FILTERS), F32),
            jax.ShapeDtypeStruct((1, COUNT), F32),
        ),
        in_specs=[any_spec] * 3,
        out_specs=(any_spec,) * 4,
        scratch_shapes=[
            vmem((FEATS, HIDDEN), BF16),
            vmem((FEATS, HIDDEN), F32),
            vmem((2, SMALL, 128), BF16),
            vmem((2, SMALL, 128), F32),
            pltpu.SemaphoreType.DMA((STEPS + 1,)),
            pltpu.SemaphoreType.DMA((STEPS + 5,)),
        ],
        compiler_params=pltpu.CompilerParams(vmem_limit_bytes=56 * 2**20),
    )(big, small, loss)
    return (loss.reshape(COUNT), g_mix, g_in, g_out)


def solution(mesh):
    placed = (P(("blk", "dp"), None, None), P(), P(), P(), P(("blk", "dp")), P(("blk", "dp")))
    return jax.shard_map(
        on_device,
        mesh=mesh,
        in_specs=placed,
        out_specs=(P(("blk", "dp")), P(), P(), P()),
        check_vma=False,
    )
```
